256 devices in a mesh: seq: 64 (over y, x, z_hi), cand: 4 (over z_lo, core).
Axes of the slice: x: 4, y: 4, z: 8 (z_hi: 4, z_lo: 2; z = z_hi * 2 + z_lo), core: 2. Of those that a mesh axis runs over, the one named last changes fastest.
Arguments:
- history_embed: bfloat16 [32768, 512], P('seq'), may hold values from -6 to 6
- candidate_embed: bfloat16 [2048, 512], P(('seq', 'cand')), may hold values from -6 to 6
- query_weight: bfloat16 [512, 512], replicated, may hold values from -0.25 to 0.25
- unit_weight: bfloat16 [512, 512], replicated, may hold values from -0.25 to 0.25
- keyval_weight: bfloat16 [512, 1024], replicated, may hold values from -0.25 to 0.25
- output_weight: bfloat16 [512, 512], replicated, may hold values from -0.25 to 0.25
- block_user: int32 [64], P('seq'), may hold values from 0 to 1, as said below
- block_length: int32 [64], P('seq'), may hold values from 128 to 512, as said below
- candidate_user: int32 [2048], P(('seq', 'cand')), may hold values from 0 to 1
- grad_output: bfloat16 [2048, 512], P(('seq', 'cand')), may hold values from -6 to 6
Outputs:
- candidate_output: bfloat16 [2048, 512], P(('seq', 'cand'))
- history_grad: bfloat16 [32768, 512], P('seq')
- candidate_grad: bfloat16 [2048, 512], P(('seq', 'cand'))
The draws below stay inside these ranges and needn't reach their ends.
Inputs may be any that keep to these rules, and one draw needn't show every extreme that they name: block_user never falls from one block to the next; each of the 2 users owns at least one block. block_length is a multiple of 128; the valid events of a block are its first block_length ones; some block is full.
All inputs are finite; a program needn't handle non-finite values.
Results may differ from the reference program's by a relative error of at most 0.008.
Values may be sent and summed in bfloat16 or wider, within the bound.
No kernel may reach another device: no remote copies, remote signals or barrier semaphores. Data moves between devices by JAX's collectives and lax.ppermute only.
A program may use at most 64 MiB of HBM per device.

```python
import jax
import jax.numpy as jnp
from jax import lax

D = 512
HEADS = 8
HEAD_DIM = 64
BLOCK = 512
TILE = 128
USERS = 2
NBLK = 64
HIST = 32768
CANDS = 2048


def draw_block_user(key, part):
    key = jax.random.fold_in(key, 11)
    shuffled = jax.random.permutation(key, NBLK - 1)
    boundaries = shuffled[:USERS - 1] + 1
    block_index = jnp.arange(NBLK, dtype=jnp.int32)
    return jnp.sum((block_index[:, None] >= boundaries[None, :]).astype(jnp.int32), axis=1).astype(jnp.int32)


def draw_block_length(key, part):
    key = jax.random.fold_in(key, 23)
    key_units, key_full = jax.random.split(key)
    tile_units = jax.random.randint(key_units, (NBLK,), 1, BLOCK // TILE + 1)
    fullest = jax.random.randint(key_full, (), 0, NBLK)
    block_index = jnp.arange(NBLK, dtype=jnp.int32)
    return (jnp.where(block_index == fullest, BLOCK // TILE, tile_units) * TILE).astype(jnp.int32)


def place_ends(entries, stream_key, least, top_value):
    longest = entries.shape.index(max(entries.shape))
    spots = []
    for shift in (0, 1):
        where = [jax.random.randint(jax.random.fold_in(stream_key, axis), (), 0, length) for axis, length in enumerate(entries.shape)]
        where[longest] = (where[longest] + shift) % entries.shape[longest]
        spots.append(tuple(where))
    return entries.at[spots[0]].set(least).at[spots[1]].set(top_value)


def shard_levels(key, dims, pieces, smallest, high):
    def one(axis_at, blocks):
        heights = jax.random.uniform(jax.random.fold_in(jax.random.fold_in(key, 6), axis_at), (blocks,), jnp.float32, smallest / len(pieces), high / len(pieces))
        return jnp.repeat(jnp.exp(heights), dims[axis_at] // blocks).reshape((-1,) + (1,) * (len(dims) - axis_at - 1))

    factor_of = one(*pieces[0])
    for cut in pieces[1:]:
        factor_of = factor_of * one(*cut)
    return factor_of


def bell_draw(stream_key, extent, spread, bound, shards=(), kind=jnp.bfloat16):
    result = jax.random.normal(stream_key, extent, jnp.float32) * spread
    if len(shards) > 0:
        result = shard_levels(stream_key, extent, shards, -0.22, 0.18) * result
    return jnp.clip(result, min=-bound, max=bound).astype(kind)


def setup_inputs(seed: int = 0) -> dict:
    key_of = jax.random.split(jax.random.key(seed), 11)
    return {
        "history_embed": bell_draw(key_of[0], (HIST, D), 1.0, 6.0, ((0, 64),)),
        "candidate_embed": bell_draw(key_of[1], (CANDS, D), 1.0, 6.0, ((0, 256),)),
        "query_weight": bell_draw(key_of[2], (D, D), D ** -0.5, 0.25),
        "unit_weight": bell_draw(key_of[3], (D, D), D ** -0.5, 0.25),
        "keyval_weight": bell_draw(key_of[4], (D, 2 * D), D ** -0.5, 0.25),
        "output_weight": bell_draw(key_of[5], (D, D), D ** -0.5, 0.25),
        "block_user": draw_block_user(jax.random.fold_in(key_of[10], 71), 0),
        "block_length": draw_block_length(jax.random.fold_in(key_of[10], 71), 0),
        "candidate_user": place_ends(jax.random.randint(key_of[8], (CANDS,), 0, USERS), jax.random.fold_in(key_of[8], 1), 0, USERS - 1).astype(jnp.int32),
        "grad_output": bell_draw(key_of[9], (CANDS, D), 1.0, 6.0, ((0, 256),)),
    }


def rounded(values):
    return lax.optimization_barrier(values.astype(jnp.bfloat16))

def silu_slope(linear):
    sigmoid_part = jax.nn.sigmoid(linear)
    return sigmoid_part * (1.0 + linear * (1.0 - sigmoid_part))

def reference(history_embed, candidate_embed, query_weight, unit_weight, keyval_weight, output_weight, block_user, block_length, candidate_user, grad_output):
    score_scale = HEAD_DIM ** (-0.5)
    query = rounded(jnp.dot(candidate_embed, query_weight, preferred_element_type=jnp.float32))
    unit_linear = jnp.dot(candidate_embed, unit_weight, preferred_element_type=jnp.float32)
    unit_gate = rounded(jax.nn.silu(unit_linear))
    keyval = rounded(jnp.dot(history_embed, keyval_weight, preferred_element_type=jnp.float32))
    block_rows = keyval.reshape(NBLK, BLOCK, 2 * D)
    query_heads = query.astype(jnp.float32).reshape(CANDS, HEADS, HEAD_DIM)
    position = jnp.arange(BLOCK, dtype=jnp.int32)

    def block_parts(inputs):
        rows_here, owner, length = inputs
        key_heads = rows_here[:, :D].astype(jnp.float32).reshape(BLOCK, HEADS, HEAD_DIM)
        value_heads = rows_here[:, D:].astype(jnp.float32).reshape(BLOCK, HEADS, HEAD_DIM)
        live_mask = ((candidate_user[:, None] == owner) & (position[None, :] < length)).astype(jnp.float32)[:, None, :]
        scores = jnp.einsum('chd,thd->cht', query_heads, key_heads) * score_scale
        return (key_heads, value_heads, live_mask, scores)

    def forward_block(running, inputs):
        key_heads, value_heads, live_mask, scores = block_parts(inputs)
        weights = rounded(jax.nn.silu(scores) * live_mask).astype(jnp.float32)
        return (running + jnp.einsum('cht,thd->chd', weights, value_heads).reshape(CANDS, D), None)
    attention, _ = lax.scan(forward_block, jnp.zeros((CANDS, D), jnp.float32), (block_rows, block_user, block_length))
    row_mean = lax.optimization_barrier(jnp.mean(attention, axis=1, keepdims=True))
    centered = attention - row_mean
    inverse = lax.rsqrt(lax.optimization_barrier(jnp.mean(centered * centered, axis=1, keepdims=True)) + 1e-05)
    normed = centered * inverse
    gated = rounded(normed * unit_gate.astype(jnp.float32))
    candidate_output = (candidate_embed.astype(jnp.float32) + jnp.dot(gated, output_weight, preferred_element_type=jnp.float32)).astype(jnp.bfloat16)
    d_gated = jnp.dot(grad_output, output_weight.T, preferred_element_type=jnp.float32)
    grad_normed = d_gated * unit_gate.astype(jnp.float32)
    d_attention = rounded(inverse * (grad_normed - lax.optimization_barrier(jnp.mean(grad_normed, axis=1, keepdims=True)) - normed * lax.optimization_barrier(jnp.mean(grad_normed * normed, axis=1, keepdims=True))))
    d_unit = rounded(d_gated * normed * silu_slope(unit_linear))
    grad_heads = d_attention.astype(jnp.float32).reshape(CANDS, HEADS, HEAD_DIM)

    def backward_block(running, inputs):
        key_heads, value_heads, live_mask, scores = block_parts(inputs)
        weights = rounded(jax.nn.silu(scores) * live_mask).astype(jnp.float32)
        grad_weights = jnp.einsum('chd,thd->cht', grad_heads, value_heads)
        d_scores = rounded(grad_weights * silu_slope(scores) * live_mask * score_scale).astype(jnp.float32)
        query_part = jnp.einsum('cht,thd->chd', d_scores, key_heads).reshape(CANDS, D)
        key_part = jnp.einsum('cht,chd->thd', d_scores, query_heads).reshape(BLOCK, D)
        value_part = jnp.einsum('cht,chd->thd', weights, grad_heads).reshape(BLOCK, D)
        return (running + query_part, jnp.concatenate([key_part, value_part], axis=1))
    d_query, d_blocks = lax.scan(backward_block, jnp.zeros((CANDS, D), jnp.float32), (block_rows, block_user, block_length))
    d_keyval = d_blocks.reshape(HIST, 2 * D)
    weight_full = keyval_weight.astype(jnp.float32)
    history_grad = jnp.dot(d_keyval, weight_full.T, precision=lax.Precision.HIGHEST, preferred_element_type=jnp.float32).astype(jnp.bfloat16)
    d_query_low = d_query.astype(jnp.bfloat16)
    candidate_grad = (grad_output.astype(jnp.float32) + jnp.dot(d_query_low, query_weight.T, preferred_element_type=jnp.float32) + jnp.dot(d_unit, unit_weight.T, preferred_element_type=jnp.float32)).astype(jnp.bfloat16)
    return (candidate_output, history_grad, candidate_grad)
```

```python
from functools import partial

import jax
import jax.numpy as jnp
from jax import lax
from jax.experimental import pallas as pl
from jax.experimental.pallas import tpu as pltpu
from jax.sharding import PartitionSpec as P

HEADS = 8
PAIRS = 4
LANES = 128
F32 = jnp.float32
BF16 = jnp.bfloat16
VMEM_BYTES = 48 * 1024 * 1024


def nn(a, b):
    return lax.dot_general(a, b, (((1,), (0,)), ((), ())), preferred_element_type=F32)


def nt(a, b):
    return lax.dot_general(a, b, (((1,), (1,)), ((), ())), preferred_element_type=F32)


def call(body, outs, scratch=(), smem=(), count=0, flops=0):
    spec = pl.BlockSpec(memory_space=pltpu.VMEM)
    sspec = pl.BlockSpec(memory_space=pltpu.SMEM)
    return pl.pallas_call(
        body,
        out_shape=outs,
        in_specs=[sspec if i in smem else spec for i in range(count)],
        out_specs=jax.tree.map(lambda _: spec, outs),
        scratch_shapes=list(scratch),
        compiler_params=pltpu.CompilerParams(vmem_limit_bytes=VMEM_BYTES),
        cost_estimate=pl.CostEstimate(flops=flops, bytes_accessed=1 << 20, transcendentals=0),
    )


def keyval_kernel(length_ref, hist_ref, weight_ref, key_ref, value_ref):
    events = hist_ref.shape[0]
    keyval = nn(hist_ref[...], weight_ref[...])
    row = lax.broadcasted_iota(jnp.int32, (events, LANES), 0)
    lane = lax.broadcasted_iota(jnp.int32, (events, LANES), 1)
    live = row < length_ref[0]
    half = LANES // 2
    for p in range(PAIRS):
        for ref, base in ((key_ref, 0), (value_ref, PAIRS * LANES)):
            part = keyval[:, base + p * LANES : base + (p + 1) * LANES]
            ref[p, :events, :] = jnp.where(live & (lane < half), part, 0.0).astype(BF16)
            ref[p, events:, :] = jnp.where(live & (lane >= half), part, 0.0).astype(BF16)


def forward_kernel(user_ref, pay_ref, weight_ref, key_ref, value_ref, query_ref, att_ref):
    rows, width = query_ref.shape
    chunk = 128
    owner = user_ref[0].astype(F32)

    def step(i, carry):
        r = pl.ds(pl.multiple_of(i * chunk, chunk), chunk)
        pay = pay_ref[r, :]
        mine = pay[:, width : width + 1].astype(F32) == owner
        query = nn(pay[:, :width], weight_ref[...]).astype(BF16).astype(F32)
        scaled = jnp.where(mine, query * 0.0625, 0.0).astype(BF16)
        query_ref[r, :] = scaled
        for p in range(PAIRS):
            cols = slice(p * LANES, (p + 1) * LANES)
            u = nt(scaled[:, cols], key_ref[p])
            w = (u + u * jnp.tanh(u)).astype(BF16)
            att_ref[r, cols] = nn(w, value_ref[p]).astype(BF16)
        return carry

    lax.fori_loop(0, rows // chunk, step, 0)


def slope_kernel(query_ref, key_ref, slope_ref, slope_t_ref, weight_t_ref):
    rows = query_ref.shape[0]
    both = key_ref.shape[1]
    chunk = 128

    def one(u):
        t = jnp.tanh(u)
        return t, (1.0 + t) + u * (1.0 - t * t)

    for p in range(PAIRS):
        cols = slice(p * LANES, (p + 1) * LANES)

        def step(i, carry, p=p, cols=cols):
            r = pl.ds(pl.multiple_of(i * chunk, chunk), chunk)
            u = nt(query_ref[r, cols], key_ref[p])
            slope_ref[p, r, :] = one(u)[1].astype(BF16)
            return carry

        lax.fori_loop(0, rows // chunk, step, 0)

        def step_t(i, carry, p=p, cols=cols):
            r = pl.ds(pl.multiple_of(i * chunk, chunk), chunk)
            u = nt(key_ref[p, r, :], query_ref[:, cols])
            t, slope = one(u)
            slope_t_ref[p, r, :] = slope.astype(BF16)
            weight_t_ref[p, r, :] = (u + u * t).astype(BF16)
            return carry

        lax.fori_loop(0, both // chunk, step_t, 0)


def own_kernel(pay_ref, grad_ref, unit_ref, out_ref, gate_ref, uslope_ref, dgated_ref):
    width = grad_ref.shape[1]
    linear = nn(pay_ref[...][:, :width], unit_ref[...])
    sig = jax.nn.sigmoid(linear)
    gate_ref[...] = (linear * sig).astype(BF16).astype(F32)
    uslope_ref[...] = sig * (1.0 + linear * (1.0 - sig))
    dgated_ref[...] = nt(grad_ref[...], out_ref[...])


def norm_kernel(part_ref, gate_ref, dgated_ref, uslope_ref, datt_ref, gated_ref, dunit_ref):
    own, width = gate_ref.shape
    total = part_ref.shape[0]
    att = jnp.sum(part_ref[...].astype(F32).reshape(total // own, own, width), axis=0)
    mean = jnp.mean(att, axis=1, keepdims=True)
    centered = att - mean
    inverse = lax.rsqrt(jnp.mean(centered * centered, axis=1, keepdims=True) + 1e-05)
    normed = centered * inverse
    gate = gate_ref[...]
    dgated = dgated_ref[...]
    g = dgated * gate
    datt = inverse * (
        g
        - jnp.mean(g, axis=1, keepdims=True)
        - normed * jnp.mean(g * normed, axis=1, keepdims=True)
    )
    datt_ref[...] = datt.astype(BF16)
    gated_ref[...] = (normed * gate).astype(BF16)
    dunit_ref[...] = (dgated * normed * uslope_ref[...]).astype(BF16)


def output_kernel(embed_ref, grad_ref, gated_ref, dunit_ref, out_ref, unit_ref, result_ref, base_ref):
    result_ref[...] = (embed_ref[...].astype(F32) + nn(gated_ref[...], out_ref[...])).astype(BF16)
    base_ref[...] = grad_ref[...].astype(F32) + nt(dunit_ref[...], unit_ref[...])


def backward_kernel(user_ref, pay_ref, datt_ref, key_ref, value_ref, slope_ref, masked_ref, dq_ref):
    rows, width = datt_ref.shape
    chunk = 128
    owner = user_ref[0].astype(F32)

    def step(i, carry):
        r = pl.ds(pl.multiple_of(i * chunk, chunk), chunk)
        mine = pay_ref[r, width : width + 1].astype(F32) == owner
        datt = jnp.where(mine, datt_ref[r, :].astype(F32), 0.0).astype(BF16)
        masked_ref[r, :] = datt
        for p in range(PAIRS):
            cols = slice(p * LANES, (p + 1) * LANES)
            dw = nt(datt[:, cols], value_ref[p])
            ds = (dw * slope_ref[p, r, :].astype(F32)).astype(BF16)
            dq_ref[r, cols] = nn(ds, key_ref[p]).astype(BF16)
        return carry

    lax.fori_loop(0, rows // chunk, step, 0)


def keyval_grad_kernel(
    query_ref, datt_ref, value_ref, slope_t_ref, weight_t_ref, kvw_ref, grad_ref, dkv_ref
):
    events = value_ref.shape[1] // 2
    width = datt_ref.shape[1]
    chunk = 128
    low = lax.broadcasted_iota(jnp.int32, (chunk, LANES), 1) < LANES // 2

    def step(i, carry):
        r = pl.ds(pl.multiple_of(i * chunk, chunk), chunk)
        r2 = pl.ds(pl.multiple_of(events + i * chunk, chunk), chunk)
        for p in range(PAIRS):
            cols = slice(p * LANES, (p + 1) * LANES)
            datt = datt_ref[:, cols]
            query = query_ref[:, cols]
            dks, dvs = [], []
            for rr in (r, r2):
                dw = nt(value_ref[p, rr, :], datt)
                ds = (dw * slope_t_ref[p, rr, :].astype(F32)).astype(BF16)
                dks.append(nn(ds, query))
                dvs.append(nn(weight_t_ref[p, rr, :], datt))
            dkv_ref[r, cols] = jnp.where(low, dks[0], dks[1]).astype(BF16)
            vcols = slice(width + p * LANES, width + (p + 1) * LANES)
            dkv_ref[r, vcols] = jnp.where(low, dvs[0], dvs[1]).astype(BF16)
        grad_ref[r, :] = nt(dkv_ref[r, :], kvw_ref[...]).astype(BF16)
        return carry

    lax.fori_loop(0, events // chunk, step, 0)


def final_kernel(part_ref, base_ref, weight_ref, result_ref):
    own, width = base_ref.shape
    total = part_ref.shape[0]
    dq = jnp.sum(part_ref[...].astype(F32).reshape(total // own, own, width), axis=0) * 0.0625
    result_ref[...] = (base_ref[...] + nt(dq.astype(BF16), weight_ref[...])).astype(BF16)


def shards(
    history_embed,
    candidate_embed,
    query_weight,
    unit_weight,
    keyval_weight,
    output_weight,
    block_user,
    block_length,
    candidate_user,
    grad_output,
):
    own, width = candidate_embed.shape
    events = history_embed.shape[0]
    groups = lax.axis_size("seq")
    rows = own * groups
    s = jax.ShapeDtypeStruct

    user = jnp.broadcast_to(candidate_user.astype(BF16)[:, None], (own, LANES))
    pay = jnp.concatenate([candidate_embed, user], axis=1)
    pay_all = lax.all_to_all(
        jnp.broadcast_to(pay, (groups, own, width + LANES)), "seq", 0, 0
    ).reshape(rows, width + LANES)

    wide = s((PAIRS, 2 * events, LANES), BF16)
    keys, values = call(keyval_kernel, [wide, wide], smem=(0,), count=3, flops=1 << 30)(
        block_length, history_embed, keyval_weight
    )
    own_f32 = s((own, width), F32)
    own_b16 = s((own, width), BF16)
    gate, uslope, dgated = call(own_kernel, [own_f32] * 3, count=4, flops=1 << 26)(
        candidate_embed, grad_output, unit_weight, output_weight
    )
    big = s((rows, width), BF16)
    query, att = call(forward_kernel, [big, big], smem=(0,), count=5, flops=1 << 31)(
        block_user, pay_all, query_weight, keys, values
    )
    att_all = lax.all_to_all(att.reshape(groups, own, width), "seq", 0, 0).reshape(rows, width)
    slope, slope_t, weight_t = call(
        slope_kernel,
        [
            s((PAIRS, rows, 2 * events), BF16),
            s((PAIRS, 2 * events, rows), BF16),
            s((PAIRS, 2 * events, rows), BF16),
        ],
        count=2,
        flops=1 << 32,
    )(query, keys)
    datt, gated, dunit = call(norm_kernel, [own_b16] * 3, count=4, flops=1 << 20)(
        att_all, gate, dgated, uslope
    )
    datt_all = lax.all_to_all(
        jnp.broadcast_to(datt, (groups, own, width)), "seq", 0, 0
    ).reshape(rows, width)
    candidate_output, base = call(output_kernel, [own_b16, own_f32], count=6, flops=1 << 26)(
        candidate_embed, grad_output, gated, dunit, output_weight, unit_weight
    )
    masked, dq = call(backward_kernel, [big, big], smem=(0,), count=6, flops=1 << 31)(
        block_user, pay_all, datt_all, keys, values, slope
    )
    dq_all = lax.all_to_all(dq.reshape(groups, own, width), "seq", 0, 0).reshape(rows, width)
    hist_part = call(
        keyval_grad_kernel,
        s((events, width), BF16),
        scratch=[pltpu.VMEM((events, 2 * width), BF16)],
        count=6,
        flops=1 << 32,
    )(query, masked, values, slope_t, weight_t, keyval_weight)

    cand = lax.axis_index("cand")
    core = cand % 2
    half = events // 2
    mine = lax.dynamic_slice_in_dim(hist_part, core * half, half, 0)
    other = lax.dynamic_slice_in_dim(hist_part, (1 - core) * half, half, 0)
    swap_core = [(i, i ^ 1) for i in range(4)]
    swap_chip = [(i, i ^ 2) for i in range(4)]
    got = lax.ppermute(other, "cand", swap_core)
    pair = (mine.astype(F32) + got.astype(F32)).astype(BF16)
    got = lax.ppermute(pair, "cand", swap_chip)
    quad = (pair.astype(F32) + got.astype(F32)).astype(BF16)
    got = lax.ppermute(quad, "cand", swap_core)
    history_grad = jnp.where(
        core == 0,
        jnp.concatenate([quad, got], axis=0),
        jnp.concatenate([got, quad], axis=0),
    )
    candidate_grad = call(final_kernel, own_b16, count=3, flops=1 << 26)(
        dq_all, base, query_weight
    )
    return (candidate_output, history_grad, candidate_grad)


def solution(mesh):
    in_specs = (
        P("seq", None),
        P(("seq", "cand"), None),
        P(),
        P(),
        P(),
        P(),
        P("seq"),
        P("seq"),
        P(("seq", "cand")),
        P(("seq", "cand"), None),
    )
    out_specs = (P(("seq", "cand"), None), P("seq", None), P(("seq", "cand"), None))
    return jax.shard_map(shards, mesh=mesh, in_specs=in_specs, out_specs=out_specs, check_vma=False)
```

```python
import jax
import jax.numpy as jnp
from jax import lax
from jax.experimental import pallas as pl
from jax.experimental.pallas import tpu as pltpu
from jax.sharding import Mesh, PartitionSpec as P

HEADS = 8
PAIRS = 4
LANES = 128
F32 = jnp.float32
BF16 = jnp.bfloat16
SMALL = 8 * 1024 * 1024
WHOLE = 65600000
HIGH = 4
STEP = 256


def nn(a, b):
    return lax.dot_general(a, b, (((1,), (0,)), ((), ())), preferred_element_type=F32)


def nt(a, b):
    return lax.dot_general(a, b, (((1,), (1,)), ((), ())), preferred_element_type=F32)


def call(body, ins, outs, scratch=(), flops=0, limit=SMALL):
    place = {"v": pltpu.VMEM, "s": pltpu.SMEM, "h": pltpu.HBM}
    spec = [pl.BlockSpec(memory_space=place[i]) for i in ins]
    shapes = [shape for shape, _ in outs]
    out_spec = [pl.BlockSpec(memory_space=place[i]) for _, i in outs]
    return pl.pallas_call(
        body,
        out_shape=shapes,
        in_specs=spec,
        out_specs=out_spec,
        scratch_shapes=list(scratch),
        compiler_params=pltpu.CompilerParams(vmem_limit_bytes=limit),
        cost_estimate=pl.CostEstimate(flops=flops, bytes_accessed=1 << 20, transcendentals=0),
    )


def start(sems, *pairs):
    copies = [pltpu.make_async_copy(src, dst, sems.at[i]) for i, (src, dst) in enumerate(pairs)]
    for copy in copies:
        copy.start()
    return copies


def pack_kernel(user_hbm, embed_hbm, grad_hbm, out_ref, user_ref, embed_ref, grad_ref, sems):
    copies = start(sems, (user_hbm, user_ref), (embed_hbm, embed_ref), (grad_hbm, grad_ref))
    for copy in copies:
        copy.wait()
    own, width = embed_ref.shape
    row = lax.broadcasted_iota(jnp.int32, (own, own), 0)
    lane = lax.broadcasted_iota(jnp.int32, (own, own), 1)
    user = jnp.broadcast_to(user_ref[...].astype(F32), (own, own))
    user = jnp.sum(jnp.where(row == lane, user, 0.0), axis=1, keepdims=True)
    out_ref[:, :width] = embed_ref[...]
    out_ref[:, width : width + LANES] = jnp.broadcast_to(user, (own, LANES)).astype(BF16)
    out_ref[:, width + LANES :] = grad_ref[...]


def spread_kernel(own_ref, one_ref, two_ref, three_ref, after_hbm, column_ref, plane_ref):
    refs = (own_ref, one_ref, two_ref, three_ref)
    column = jnp.concatenate([r[...].astype(F32) for r in refs], axis=0).astype(BF16)
    column_ref[...] = column
    for i in range(plane_ref.shape[0]):
        plane_ref[i] = column[:, : plane_ref.shape[2]]


def keyval_kernel(length_ref, hist_ref, weight_ref, key_ref, value_ref):
    events = hist_ref.shape[0]
    keyval = nn(hist_ref[...], weight_ref[...])
    row = lax.broadcasted_iota(jnp.int32, (events, LANES), 0)
    lane = lax.broadcasted_iota(jnp.int32, (events, LANES), 1)
    live = row < length_ref[0]
    half = LANES // 2
    for p in range(PAIRS):
        for ref, base in ((key_ref, 0), (value_ref, PAIRS * LANES)):
            part = keyval[:, base + p * LANES : base + (p + 1) * LANES]
            ref[p, :events, :] = jnp.where(live & (lane < half), part, 0.0).astype(BF16)
            ref[p, events:, :] = jnp.where(live & (lane >= half), part, 0.0).astype(BF16)


def forward_kernel(user_ref, pay_ref, weight_ref, key_ref, value_ref, query_ref, att_ref):
    rows, width = query_ref.shape
    pay = pay_ref[...]
    mine = pay[:, width : width + 1].astype(F32) == user_ref[0].astype(F32)
    query = nn(pay[:, :width], weight_ref[...]).astype(BF16).astype(F32)
    query_ref[...] = jnp.where(mine, query * 0.0625, 0.0).astype(BF16)
    for p in range(PAIRS):
        cols = slice(p * LANES, (p + 1) * LANES)
        for r in range(0, rows, STEP):
            r = slice(r, r + STEP)
            u = nt(query_ref[r, cols], key_ref[p])
            w = (u + u * jnp.tanh(u)).astype(BF16)
            att_ref[r, cols] = nn(w, value_ref[p]).astype(BF16)


def own_kernel(pay_ref, unit_ref, out_ref, gate_ref, uslope_ref, dgated_ref):
    width = unit_ref.shape[0]
    pay = pay_ref[...]
    linear = nn(pay[:, :width], unit_ref[...])
    sig = jax.nn.sigmoid(linear)
    gate_ref[...] = (linear * sig).astype(BF16).astype(F32)
    uslope_ref[...] = sig * (1.0 + linear * (1.0 - sig))
    dgated_ref[...] = nt(pay[:, width + LANES :], out_ref[...])


def sum_kernel(part_ref, out_ref):
    own, width = out_ref.shape
    parts = part_ref.shape[0] // own
    total = jnp.sum(part_ref[...].astype(F32).reshape(parts, own, width), axis=0)
    out_ref[...] = total.astype(out_ref.dtype)


def norm_kernel(
    own_ref, one_ref, two_ref, three_ref, gate_ref, dgated_ref, uslope_ref, datt_ref, gated_ref, dunit_ref
):
    own, width = gate_ref.shape
    block = own // HIGH
    att = own_ref[...].astype(F32)
    for k, ref in ((1, one_ref), (2, two_ref), (3, three_ref)):
        part = ref[...].astype(F32)
        att = att + jnp.concatenate([part[(HIGH - k) * block :], part[: (HIGH - k) * block]], axis=0)
    mean = jnp.mean(att, axis=1, keepdims=True)
    centered = att - mean
    inverse = lax.rsqrt(jnp.mean(centered * centered, axis=1, keepdims=True) + 1e-05)
    normed = centered * inverse
    gate = gate_ref[...]
    dgated = dgated_ref[...]
    g = dgated * gate
    datt = inverse * (
        g
        - jnp.mean(g, axis=1, keepdims=True)
        - normed * jnp.mean(g * normed, axis=1, keepdims=True)
    )
    datt = datt.astype(BF16)
    for i in range(datt_ref.shape[0]):
        datt_ref[i] = datt
    gated_ref[...] = (normed * gate)[:block].astype(BF16)
    dunit_ref[...] = (dgated * normed * uslope_ref[...])[:block].astype(BF16)


def output_kernel(embed_ref, grad_ref, gated_ref, dunit_ref, out_ref, unit_ref, result_ref, base_ref):
    result_ref[...] = (embed_ref[...].astype(F32) + nn(gated_ref[...], out_ref[...])).astype(BF16)
    base_ref[...] = grad_ref[...].astype(F32) + nt(dunit_ref[...], unit_ref[...])


def silu_pair(u):
    t = jnp.tanh(u)
    return u + u * t, (1.0 + t) + u * (1.0 - t * t)


def backward_kernel(user_ref, pay_ref, query_ref, datt_ref, key_ref, value_ref, masked_ref, dq_ref):
    rows, width = datt_ref.shape
    mine = pay_ref[...][:, width : width + 1].astype(F32) == user_ref[0].astype(F32)
    masked_ref[...] = jnp.where(mine, datt_ref[...].astype(F32), 0.0).astype(BF16)
    for p in range(PAIRS):
        cols = slice(p * LANES, (p + 1) * LANES)
        for r in range(0, rows, STEP):
            r = slice(r, r + STEP)
            slope = silu_pair(nt(query_ref[r, cols], key_ref[p]))[1]
            ds = (nt(masked_ref[r, cols], value_ref[p]) * slope).astype(BF16)
            dq_ref[r, cols] = nn(ds, key_ref[p]).astype(BF16)


def keyval_grad_kernel(
    core_ref, query_ref, datt_ref, key_ref, value_ref, kvw_ref, mine_ref, other_ref, dkv_ref
):
    events = value_ref.shape[1] // 2
    width = datt_ref.shape[1]
    low = lax.broadcasted_iota(jnp.int32, (events, LANES), 1) < LANES // 2
    for p in range(PAIRS):
        cols = slice(p * LANES, (p + 1) * LANES)
        vcols = slice(width + p * LANES, width + (p + 1) * LANES)
        datt = datt_ref[:, cols]
        query = query_ref[:, cols]
        dks, dvs = [], []
        for r in (slice(0, events), slice(events, 2 * events)):
            weight, slope = silu_pair(nt(key_ref[p, r, :], query))
            ds = (nt(value_ref[p, r, :], datt) * slope).astype(BF16)
            dks.append(nn(ds, query))
            dvs.append(nn(weight.astype(BF16), datt))
        dkv_ref[:, cols] = jnp.where(low, dks[0], dks[1]).astype(BF16)
        dkv_ref[:, vcols] = jnp.where(low, dvs[0], dvs[1]).astype(BF16)
    half = events // 2
    core = core_ref[0]
    mine = pl.ds(pl.multiple_of(core * half, half), half)
    other = pl.ds(pl.multiple_of((1 - core) * half, half), half)
    other_ref[...] = nt(dkv_ref[other, :], kvw_ref[...]).astype(BF16)
    mine_ref[...] = nt(dkv_ref[mine, :], kvw_ref[...])


def add_kernel(one_ref, two_ref, *rest):
    rest[-1][...] = (one_ref[...].astype(F32) + two_ref[...].astype(F32)).astype(BF16)


def final_kernel(own_ref, one_ref, two_ref, three_ref, base_ref, weight_ref, result_ref):
    dq = (own_ref[...] + one_ref[...]) + (two_ref[...] + three_ref[...])
    dq = (dq * 0.0625).astype(BF16)
    result_ref[...] = (base_ref[...] + nt(dq, weight_ref[...])).astype(BF16)


def shards(
    history_embed,
    candidate_embed,
    query_weight,
    unit_weight,
    keyval_weight,
    output_weight,
    block_user,
    block_length,
    candidate_user,
    grad_output,
):
    own, width = candidate_embed.shape
    events = history_embed.shape[0]
    plane = lax.axis_size("plane")
    column = own * HIGH
    rows = column * plane
    s = jax.ShapeDtypeStruct

    def from_up(value, k):
        return lax.ppermute(value, "high", [((i + k) % HIGH, i) for i in range(HIGH)])

    def exchange(value):
        parts = value.reshape(plane, column, value.shape[-1])
        return lax.all_to_all(parts, "plane", 0, 0).reshape(rows, value.shape[-1])

    sems = pltpu.SemaphoreType.DMA
    full = width + LANES + width
    pack = call(
        pack_kernel,
        "hhh",
        [(s((own, full), BF16), "v")],
        [pltpu.VMEM((1, own), jnp.int32), pltpu.VMEM((own, width), BF16), pltpu.VMEM((own, width), BF16), sems((3,))],
        limit=WHOLE,
    )(candidate_user.reshape(1, own), candidate_embed, grad_output)[0]
    wide = (s((PAIRS, 2 * events, LANES), BF16), "v")
    keys, values = call(keyval_kernel, "svv", [wide, wide], flops=1 << 30)(
        block_length, history_embed, keyval_weight
    )
    pay, spread = call(
        spread_kernel,
        "vvvvh",
        [(s((column, full), BF16), "v"), (s((plane, column, width + LANES), BF16), "v")],
    )(pack, *[from_up(pack, k) for k in (1, 2, 3)], keys)
    pay_all = exchange(spread)

    col_f32 = (s((column, width), F32), "v")
    col_b16 = (s((column, width), BF16), "v")
    own_f32 = (s((own, width), F32), "v")
    own_b16 = (s((own, width), BF16), "v")
    big = (s((rows, width), BF16), "v")
    gate, uslope, dgated = call(own_kernel, "vvv", [col_f32] * 3, flops=1 << 26)(
        pay, unit_weight, output_weight
    )
    query, att = call(forward_kernel, "svvvv", [big, big], flops=1 << 31)(
        block_user, pay_all, query_weight, keys, values
    )
    att_all = exchange(att)
    att_col = call(sum_kernel, "v", [col_b16], flops=1 << 20)(att_all)[0]
    datt, gated, dunit = call(
        norm_kernel, "v" * 7, [(s((plane, column, width), BF16), "v"), own_b16, own_b16], flops=1 << 20
    )(att_col, *[from_up(att_col, k) for k in (1, 2, 3)], gate, dgated, uslope)
    datt_all = exchange(datt)
    candidate_output, base = call(output_kernel, "v" * 6, [own_b16, own_f32], flops=1 << 26)(
        candidate_embed, grad_output, gated, dunit, output_weight, unit_weight
    )
    masked, dq = call(backward_kernel, "svvvvv", [big, big], flops=1 << 31)(
        block_user, pay_all, query, datt_all, keys, values
    )
    dq_all = exchange(dq)
    dq_col = call(sum_kernel, "v", [col_f32], flops=1 << 20)(dq_all)[0]
    dq_parts = [
        lax.ppermute(
            dq_col[k * own : (k + 1) * own], "high", [(i, (i + k) % HIGH) for i in range(HIGH)]
        )
        for k in (1, 2, 3)
    ]

    half = events // 2
    core = lax.axis_index("cand") % 2
    half_b16 = (s((half, width), BF16), "v")
    mine, other = call(
        keyval_grad_kernel,
        "svvvvv",
        [(s((half, width), F32), "v"), half_b16],
        [pltpu.VMEM((events, 2 * width), BF16)],
        flops=1 << 32,
    )(core.reshape(1), query, masked, keys, values, keyval_weight)
    swap_core = [(i, i ^ 1) for i in range(4)]
    swap_chip = [(i, i ^ 2) for i in range(4)]
    got = lax.ppermute(other, "cand", swap_core)
    pair = call(add_kernel, "vvh", [half_b16])(mine, got, dq_all)[0]
    got = lax.ppermute(pair, "cand", swap_chip)
    quad = call(add_kernel, "vvhhh", [half_b16])(pair, got, *dq_parts)[0]
    got = lax.ppermute(quad, "cand", swap_core)
    history_grad = jnp.where(
        core == 0,
        jnp.concatenate([quad, got], axis=0),
        jnp.concatenate([got, quad], axis=0),
    )
    candidate_grad = call(final_kernel, "v" * 6, [own_b16], flops=1 << 26)(
        dq_col[:own], *dq_parts, base, query_weight
    )[0]
    return (candidate_output, history_grad, candidate_grad)


def solution(mesh):
    seq, cand = mesh.shape["seq"], mesh.shape["cand"]
    fine = Mesh(mesh.devices.reshape(seq // HIGH, HIGH, cand), ("plane", "high", "cand"))
    hist, full = ("plane", "high"), ("plane", "high", "cand")
    in_specs = (
        P(hist, None),
        P(full, None),
        P(),
        P(),
        P(),
        P(),
        P(hist),
        P(hist),
        P(full),
        P(full, None),
    )
    out_specs = (P(full, None), P(hist, None), P(full, None))
    return jax.shard_map(shards, mesh=fine, in_specs=in_specs, out_specs=out_specs, check_vma=False)
```

```python
import jax
import jax.numpy as jnp
from jax import lax
from jax.experimental import pallas as pl
from jax.experimental.pallas import tpu as pltpu
from jax.sharding import Mesh, PartitionSpec as P

HEADS = 8
PAIRS = 4
LANES = 128
F32 = jnp.float32
BF16 = jnp.bfloat16
SMALL = 16 * 1024 * 1024
WHOLE = 65600000
HIGH = 4
STEP = 256


def nn(a, b):
    return lax.dot_general(a, b, (((1,), (0,)), ((), ())), preferred_element_type=F32)


def nt(a, b):
    return lax.dot_general(a, b, (((1,), (1,)), ((), ())), preferred_element_type=F32)


def call(body, ins, outs, scratch=(), flops=0, limit=SMALL):
    place = {"v": pltpu.VMEM, "s": pltpu.SMEM, "h": pltpu.HBM}
    spec = [pl.BlockSpec(memory_space=place[i]) for i in ins]
    shapes = [shape for shape, _ in outs]
    out_spec = [pl.BlockSpec(memory_space=place[i]) for _, i in outs]
    return pl.pallas_call(
        body,
        out_shape=shapes,
        in_specs=spec,
        out_specs=out_spec,
        scratch_shapes=list(scratch),
        compiler_params=pltpu.CompilerParams(vmem_limit_bytes=limit),
        cost_estimate=pl.CostEstimate(flops=flops, bytes_accessed=1 << 20, transcendentals=0),
    )


def start(sems, *pairs):
    copies = [pltpu.make_async_copy(src, dst, sems.at[i]) for i, (src, dst) in enumerate(pairs)]
    for copy in copies:
        copy.start()
    return copies


def pack_kernel(user_hbm, embed_hbm, grad_hbm, out_ref, user_ref, embed_ref, grad_ref, sems):
    copies = start(sems, (user_hbm, user_ref), (embed_hbm, embed_ref), (grad_hbm, grad_ref))
    for copy in copies:
        copy.wait()
    own, width = embed_ref.shape
    row = lax.broadcasted_iota(jnp.int32, (own, own), 0)
    lane = lax.broadcasted_iota(jnp.int32, (own, own), 1)
    user = jnp.broadcast_to(user_ref[...].astype(F32), (own, own))
    user = jnp.sum(jnp.where(row == lane, user, 0.0), axis=1, keepdims=True)
    out_ref[:, :width] = embed_ref[...]
    out_ref[:, width : width + LANES] = jnp.broadcast_to(user, (own, LANES)).astype(BF16)
    out_ref[:, width + LANES :] = grad_ref[...]


def spread_kernel(own_ref, one_ref, two_ref, three_ref, *rest):
    column_ref, plane_ref = rest[-2:]
    refs = (own_ref, one_ref, two_ref, three_ref)
    column = jnp.concatenate([r[...].astype(F32) for r in refs], axis=0).astype(BF16)
    column_ref[...] = column
    for i in range(plane_ref.shape[0]):
        plane_ref[i] = column[:, : plane_ref.shape[2]]


def keyval_kernel(length_ref, hist_ref, weight_ref, key_ref, value_ref):
    events = hist_ref.shape[0]
    keyval = nn(hist_ref[...], weight_ref[...])
    row = lax.broadcasted_iota(jnp.int32, (events, LANES), 0)
    lane = lax.broadcasted_iota(jnp.int32, (events, LANES), 1)
    live = row < length_ref[0]
    half = LANES // 2
    for p in range(PAIRS):
        for ref, base in ((key_ref, 0), (value_ref, PAIRS * LANES)):
            part = keyval[:, base + p * LANES : base + (p + 1) * LANES]
            ref[p, :events, :] = jnp.where(live & (lane < half), part, 0.0).astype(BF16)
            ref[p, events:, :] = jnp.where(live & (lane >= half), part, 0.0).astype(BF16)


def forward_kernel(user_ref, pay_ref, weight_ref, key_ref, value_ref, query_ref, att_ref):
    rows, width = query_ref.shape
    pay = pay_ref[...]
    mine = pay[:, width : width + 1].astype(F32) == user_ref[0].astype(F32)
    query = nn(pay[:, :width], weight_ref[...]).astype(BF16).astype(F32)
    query_ref[...] = jnp.where(mine, query * 0.0625, 0.0).astype(BF16)
    for p in range(PAIRS):
        cols = slice(p * LANES, (p + 1) * LANES)
        for r in range(0, rows, STEP):
            r = slice(r, r + STEP)
            u = nt(query_ref[r, cols], key_ref[p])
            w = (u + u * jnp.tanh(u)).astype(BF16)
            att_ref[r, cols] = nn(w, value_ref[p]).astype(BF16)


def own_kernel(pay_ref, unit_ref, out_ref, gate_ref, uslope_ref, dgated_ref):
    width = unit_ref.shape[0]
    pay = pay_ref[...]
    linear = nn(pay[:, :width], unit_ref[...])
    sig = jax.nn.sigmoid(linear)
    gate_ref[...] = (linear * sig).astype(BF16).astype(F32)
    uslope_ref[...] = sig * (1.0 + linear * (1.0 - sig))
    dgated_ref[...] = nt(pay[:, width + LANES :], out_ref[...])


def sum_kernel(part_ref, out_ref):
    own, width = out_ref.shape
    parts = part_ref.shape[0] // own
    total = jnp.sum(part_ref[...].astype(F32).reshape(parts, own, width), axis=0)
    out_ref[...] = total.astype(out_ref.dtype)


def norm_kernel(
    own_ref, one_ref, two_ref, three_ref, gate_ref, dgated_ref, uslope_ref, datt_ref, gated_ref, dunit_ref
):
    own, width = gate_ref.shape
    block = own // HIGH
    att = own_ref[...].astype(F32)
    for k, ref in ((1, one_ref), (2, two_ref), (3, three_ref)):
        part = ref[...].astype(F32)
        att = att + jnp.concatenate([part[(HIGH - k) * block :], part[: (HIGH - k) * block]], axis=0)
    mean = jnp.mean(att, axis=1, keepdims=True)
    centered = att - mean
    inverse = lax.rsqrt(jnp.mean(centered * centered, axis=1, keepdims=True) + 1e-05)
    normed = centered * inverse
    gate = gate_ref[...]
    dgated = dgated_ref[...]
    g = dgated * gate
    datt = inverse * (
        g
        - jnp.mean(g, axis=1, keepdims=True)
        - normed * jnp.mean(g * normed, axis=1, keepdims=True)
    )
    datt = datt.astype(BF16)
    for i in range(datt_ref.shape[0]):
        datt_ref[i] = datt
    gated_ref[...] = (normed * gate)[:block].astype(BF16)
    dunit_ref[...] = (dgated * normed * uslope_ref[...])[:block].astype(BF16)


def output_kernel(embed_ref, grad_ref, gated_ref, dunit_ref, out_ref, unit_ref, result_ref, base_ref):
    result_ref[...] = (embed_ref[...].astype(F32) + nn(gated_ref[...], out_ref[...])).astype(BF16)
    base_ref[...] = grad_ref[...].astype(F32) + nt(dunit_ref[...], unit_ref[...])


def silu_pair(u):
    t = jnp.tanh(u)
    return u + u * t, (1.0 + t) + u * (1.0 - t * t)


def backward_kernel(
    user_ref, core_ref, pay_ref, query_ref, datt_ref, key_ref, value_ref, kvw_ref,
    dq_ref, mine_ref, other_ref, masked_ref, dkv_ref,
):
    width = datt_ref.shape[1]
    events = value_ref.shape[1] // 2
    owned = pay_ref[...][:, width : width + 1].astype(F32) == user_ref[0].astype(F32)
    masked_ref[...] = jnp.where(owned, datt_ref[...].astype(F32), 0.0).astype(BF16)
    low = lax.broadcasted_iota(jnp.int32, (events, LANES), 1) < LANES // 2
    for p in range(PAIRS):
        cols = slice(p * LANES, (p + 1) * LANES)
        vcols = slice(width + p * LANES, width + (p + 1) * LANES)
        datt = masked_ref[:, cols]
        query = query_ref[:, cols]
        dks, dvs, dqs = [], [], []
        for r in (slice(0, events), slice(events, 2 * events)):
            key = key_ref[p, r, :]
            weight, slope = silu_pair(nt(key, query))
            ds = (nt(value_ref[p, r, :], datt) * slope).astype(BF16)
            dks.append(nn(ds, query))
            dvs.append(nn(weight.astype(BF16), datt))
            dqs.append(nn(key.T, ds))
        dq_ref[:, cols] = (dqs[0] + dqs[1]).T.astype(BF16)
        dkv_ref[:, cols] = jnp.where(low, dks[0], dks[1]).astype(BF16)
        dkv_ref[:, vcols] = jnp.where(low, dvs[0], dvs[1]).astype(BF16)
    half = events // 2
    core = core_ref[0]
    mine = pl.ds(pl.multiple_of(core * half, half), half)
    other = pl.ds(pl.multiple_of((1 - core) * half, half), half)
    other_ref[...] = nt(dkv_ref[other, :], kvw_ref[...]).astype(BF16)
    mine_ref[...] = nt(dkv_ref[mine, :], kvw_ref[...])


def add_kernel(one_ref, two_ref, *rest):
    rest[-1][...] = (one_ref[...].astype(F32) + two_ref[...].astype(F32)).astype(BF16)


def halves_kernel(core_ref, mine_ref, other_ref, out_hbm, sems):
    half = mine_ref.shape[0]
    core = core_ref[0]
    mine = out_hbm.at[pl.ds(pl.multiple_of(core * half, half), half)]
    other = out_hbm.at[pl.ds(pl.multiple_of((1 - core) * half, half), half)]
    for copy in start(sems, (mine_ref, mine), (other_ref, other)):
        copy.wait()


def final_kernel(own_ref, one_ref, two_ref, three_ref, base_ref, weight_ref, result_ref):
    dq = (own_ref[...] + one_ref[...]) + (two_ref[...] + three_ref[...])
    dq = (dq * 0.0625).astype(BF16)
    result_ref[...] = (base_ref[...] + nt(dq, weight_ref[...])).astype(BF16)


def shards(
    history_embed,
    candidate_embed,
    query_weight,
    unit_weight,
    keyval_weight,
    output_weight,
    block_user,
    block_length,
    candidate_user,
    grad_output,
):
    own, width = candidate_embed.shape
    events = history_embed.shape[0]
    plane = lax.axis_size("plane")
    column = own * HIGH
    rows = column * plane
    s = jax.ShapeDtypeStruct

    def from_up(value, k):
        return lax.ppermute(value, "high", [((i + k) % HIGH, i) for i in range(HIGH)])

    def exchange(value):
        parts = value.reshape(plane, column, value.shape[-1])
        return lax.all_to_all(parts, "plane", 0, 0).reshape(rows, value.shape[-1])

    sems = pltpu.SemaphoreType.DMA
    full = width + LANES + width
    pack = call(
        pack_kernel,
        "hhh",
        [(s((own, full), BF16), "v")],
        [pltpu.VMEM((1, own), jnp.int32), pltpu.VMEM((own, width), BF16), pltpu.VMEM((own, width), BF16), sems((3,))],
        limit=WHOLE,
    )(candidate_user.reshape(1, own), candidate_embed, grad_output)[0]
    wide = (s((PAIRS, 2 * events, LANES), BF16), "v")
    keys, values = call(keyval_kernel, "svv", [wide, wide], flops=1 << 30)(
        block_length, history_embed, keyval_weight
    )
    core = (lax.axis_index("cand") & 1).reshape(1)
    pay, spread = call(
        spread_kernel,
        "vvvvhss",
        [(s((column, full), BF16), "v"), (s((plane, column, width + LANES), BF16), "v")],
    )(pack, *[from_up(pack, k) for k in (1, 2, 3)], keys, block_user, core)
    pay_all = exchange(spread)

    col_f32 = (s((column, width), F32), "v")
    col_b16 = (s((column, width), BF16), "v")
    own_f32 = (s((own, width), F32), "v")
    own_b16 = (s((own, width), BF16), "v")
    big = (s((rows, width), BF16), "v")
    gate, uslope, dgated = call(own_kernel, "vvv", [col_f32] * 3, flops=1 << 26)(
        pay, unit_weight, output_weight
    )
    query, att = call(forward_kernel, "svvvv", [big, big], flops=1 << 31)(
        block_user, pay_all, query_weight, keys, values
    )
    att_all = exchange(att)
    att_col = call(sum_kernel, "v", [col_b16], flops=1 << 20)(att_all)[0]
    datt, gated, dunit = call(
        norm_kernel, "v" * 7, [(s((plane, column, width), BF16), "v"), own_b16, own_b16], flops=1 << 20
    )(att_col, *[from_up(att_col, k) for k in (1, 2, 3)], gate, dgated, uslope)
    datt_all = exchange(datt)
    candidate_output, base = call(output_kernel, "v" * 6, [own_b16, own_f32], flops=1 << 26)(
        candidate_embed, grad_output, gated, dunit, output_weight, unit_weight
    )
    half = events // 2
    half_b16 = (s((half, width), BF16), "v")
    dq, mine, other = call(
        backward_kernel,
        "ssvvvvvv",
        [big, (s((half, width), F32), "v"), half_b16],
        [pltpu.VMEM((rows, width), BF16), pltpu.VMEM((events, 2 * width), BF16)],
        flops=1 << 32,
    )(block_user, core, pay_all, query, datt_all, keys, values, keyval_weight)
    dq_all = exchange(dq)
    dq_col = call(sum_kernel, "v", [col_f32], flops=1 << 20)(dq_all)[0]
    dq_parts = [
        lax.ppermute(
            dq_col[k * own : (k + 1) * own], "high", [(i, (i + k) % HIGH) for i in range(HIGH)]
        )
        for k in (1, 2, 3)
    ]

    swap_core = [(i, i ^ 1) for i in range(4)]
    swap_chip = [(i, i ^ 2) for i in range(4)]
    got = lax.ppermute(other, "cand", swap_core)
    pair = call(add_kernel, "vv", [half_b16])(mine, got)[0]
    got = lax.ppermute(pair, "cand", swap_chip)
    quad = call(add_kernel, "vv", [half_b16])(pair, got)[0]
    got = lax.ppermute(quad, "cand", swap_core)
    history_grad = call(halves_kernel, "svv", [(s((events, width), BF16), "h")], [sems((2,))])(
        core, quad, got
    )[0]
    candidate_grad = call(final_kernel, "v" * 6, [own_b16], flops=1 << 26)(
        dq_col[:own], *dq_parts, base, query_weight
    )[0]
    return (candidate_output, history_grad, candidate_grad)


def solution(mesh):
    seq, cand = mesh.shape["seq"], mesh.shape["cand"]
    fine = Mesh(mesh.devices.reshape(seq // HIGH, HIGH, cand), ("plane", "high", "cand"))
    hist, full = ("plane", "high"), ("plane", "high", "cand")
    in_specs = (
        P(hist, None),
        P(full, None),
        P(),
        P(),
        P(),
        P(),
        P(hist),
        P(hist),
        P(full),
        P(full, None),
    )
    out_specs = (P(full, None), P(hist, None), P(full, None))
    return jax.shard_map(shards, mesh=fine, in_specs=in_specs, out_specs=out_specs, check_vma=False)
```

```python
import jax
import jax.numpy as jnp
from jax import lax
from jax.experimental import pallas as pl
from jax.experimental.pallas import tpu as pltpu
from jax.sharding import Mesh, PartitionSpec as P

HEADS = 8
PAIRS = 4
LANES = 128
F32 = jnp.float32
BF16 = jnp.bfloat16
SMALL = 16 * 1024 * 1024
WHOLE = 65600000
HIGH = 4
STEP = 256


def nn(a, b):
    return lax.dot_general(a, b, (((1,), (0,)), ((), ())), preferred_element_type=F32)


def nt(a, b):
    return lax.dot_general(a, b, (((1,), (1,)), ((), ())), preferred_element_type=F32)


def call(body, ins, outs, scratch=(), flops=0, limit=SMALL):
    place = {"v": pltpu.VMEM, "s": pltpu.SMEM, "h": pltpu.HBM}
    spec = [pl.BlockSpec(memory_space=place[i]) for i in ins]
    shapes = [shape for shape, _ in outs]
    out_spec = [pl.BlockSpec(memory_space=place[i]) for _, i in outs]
    return pl.pallas_call(
        body,
        out_shape=shapes,
        in_specs=spec,
        out_specs=out_spec,
        scratch_shapes=list(scratch),
        compiler_params=pltpu.CompilerParams(vmem_limit_bytes=limit),
        cost_estimate=pl.CostEstimate(flops=flops, bytes_accessed=1 << 20, transcendentals=0),
    )


def start(sems, *pairs):
    copies = [pltpu.make_async_copy(src, dst, sems.at[i]) for i, (src, dst) in enumerate(pairs)]
    for copy in copies:
        copy.start()
    return copies


def pack_kernel(user_hbm, embed_hbm, grad_hbm, out_ref, user_ref, embed_ref, grad_ref, sems):
    copies = start(sems, (user_hbm, user_ref), (embed_hbm, embed_ref), (grad_hbm, grad_ref))
    for copy in copies:
        copy.wait()
    own, width = embed_ref.shape
    row = lax.broadcasted_iota(jnp.int32, (own, own), 0)
    lane = lax.broadcasted_iota(jnp.int32, (own, own), 1)
    user = jnp.broadcast_to(user_ref[...].astype(F32), (own, own))
    user = jnp.sum(jnp.where(row == lane, user, 0.0), axis=1, keepdims=True)
    out_ref[:, :width] = embed_ref[...]
    out_ref[:, width : width + LANES] = jnp.broadcast_to(user, (own, LANES)).astype(BF16)
    out_ref[:, width + LANES :] = grad_ref[...]


def spread_kernel(high_ref, own_ref, one_ref, two_ref, three_ref, *rest):
    column_ref, plane_ref = rest[-2:]
    refs = (own_ref, one_ref, two_ref, three_ref)
    column = jnp.concatenate([r[...].astype(F32) for r in refs], axis=0)
    column = pltpu.roll(column, high_ref[0] * own_ref.shape[0], 0).astype(BF16)
    column_ref[...] = column
    for i in range(plane_ref.shape[0]):
        plane_ref[i] = column[:, : plane_ref.shape[2]]


def keyval_kernel(length_ref, hist_ref, weight_ref, key_ref, value_ref):
    events = hist_ref.shape[0]
    keyval = nn(hist_ref[...], weight_ref[...])
    row = lax.broadcasted_iota(jnp.int32, (events, LANES), 0)
    lane = lax.broadcasted_iota(jnp.int32, (events, LANES), 1)
    live = row < length_ref[0]
    half = LANES // 2
    for p in range(PAIRS):
        for ref, base in ((key_ref, 0), (value_ref, PAIRS * LANES)):
            part = keyval[:, base + p * LANES : base + (p + 1) * LANES]
            ref[p, :events, :] = jnp.where(live & (lane < half), part, 0.0).astype(BF16)
            ref[p, events:, :] = jnp.where(live & (lane >= half), part, 0.0).astype(BF16)


def forward_kernel(user_ref, pay_ref, weight_ref, key_ref, value_ref, query_ref, att_ref):
    rows, width = query_ref.shape
    pay = pay_ref[...]
    mine = pay[:, width : width + 1].astype(F32) == user_ref[0].astype(F32)
    query = nn(pay[:, :width], weight_ref[...]).astype(BF16).astype(F32)
    query_ref[...] = jnp.where(mine, query * 0.0625, 0.0).astype(BF16)
    for p in range(PAIRS):
        cols = slice(p * LANES, (p + 1) * LANES)
        for r in range(0, rows, STEP):
            r = slice(r, r + STEP)
            u = nt(query_ref[r, cols], key_ref[p])
            w = (u + u * jnp.tanh(u)).astype(BF16)
            att_ref[r, cols] = nn(w, value_ref[p]).astype(BF16)


def own_kernel(pay_ref, unit_ref, out_ref, gate_ref, uslope_ref, dgated_ref):
    width = unit_ref.shape[0]
    pay = pay_ref[...]
    linear = nn(pay[:, :width], unit_ref[...])
    sig = jax.nn.sigmoid(linear)
    gate_ref[...] = (linear * sig).astype(BF16).astype(F32)
    uslope_ref[...] = sig * (1.0 + linear * (1.0 - sig))
    dgated_ref[...] = nt(pay[:, width + LANES :], out_ref[...])


def sum_kernel(part_ref, out_ref):
    own, width = out_ref.shape
    parts = part_ref.shape[0] // own
    total = jnp.sum(part_ref[...].astype(F32).reshape(parts, own, width), axis=0)
    out_ref[...] = total.astype(out_ref.dtype)


def norm_kernel(
    high_ref, own_ref, one_ref, two_ref, three_ref, gate_ref, dgated_ref, uslope_ref, datt_ref, gated_ref, dunit_ref
):
    own, width = gate_ref.shape
    block = own // HIGH
    refs = (own_ref, one_ref, two_ref, three_ref)
    att = sum(ref[...].astype(F32) for ref in refs)
    mean = jnp.mean(att, axis=1, keepdims=True)
    centered = att - mean
    inverse = lax.rsqrt(jnp.mean(centered * centered, axis=1, keepdims=True) + 1e-05)
    normed = centered * inverse
    gate = gate_ref[...]
    dgated = dgated_ref[...]
    g = dgated * gate
    datt = inverse * (
        g
        - jnp.mean(g, axis=1, keepdims=True)
        - normed * jnp.mean(g * normed, axis=1, keepdims=True)
    )
    datt = datt.astype(BF16)
    for i in range(datt_ref.shape[0]):
        datt_ref[i] = datt
    down = ((HIGH - high_ref[0]) & (HIGH - 1)) * block
    gated_ref[...] = pltpu.roll(normed * gate, down, 0)[:block].astype(BF16)
    dunit_ref[...] = pltpu.roll(dgated * normed * uslope_ref[...], down, 0)[:block].astype(BF16)


def output_kernel(embed_ref, grad_ref, gated_ref, dunit_ref, out_ref, unit_ref, result_ref, base_ref):
    result_ref[...] = (embed_ref[...].astype(F32) + nn(gated_ref[...], out_ref[...])).astype(BF16)
    base_ref[...] = grad_ref[...].astype(F32) + nt(dunit_ref[...], unit_ref[...])


def silu_pair(u):
    t = jnp.tanh(u)
    ut = u * t
    return u + ut, (1.0 + t) + (u - ut * t)


def backward_kernel(
    user_ref, core_ref, pay_ref, query_ref, datt_ref, key_ref, value_ref, kvw_ref,
    dq_ref, mine_ref, other_ref, masked_ref, dkv_ref,
):
    width = datt_ref.shape[1]
    events = value_ref.shape[1] // 2
    owned = pay_ref[...][:, width : width + 1].astype(F32) == user_ref[0].astype(F32)
    masked_ref[...] = jnp.where(owned, datt_ref[...].astype(F32), 0.0).astype(BF16)
    low = lax.broadcasted_iota(jnp.int32, (events, LANES), 1) < LANES // 2
    for p in range(PAIRS):
        cols = slice(p * LANES, (p + 1) * LANES)
        vcols = slice(width + p * LANES, width + (p + 1) * LANES)
        datt = masked_ref[:, cols]
        query = query_ref[:, cols]
        dks, dvs, dqs = [], [], []
        for r in (slice(0, events), slice(events, 2 * events)):
            key = key_ref[p, r, :]
            weight, slope = silu_pair(nt(key, query))
            ds = (nt(value_ref[p, r, :], datt) * slope).astype(BF16)
            dks.append(nn(ds, query))
            dvs.append(nn(weight.astype(BF16), datt))
            dqs.append(nn(key.T, ds))
        dq_ref[:, cols] = (dqs[0] + dqs[1]).T.astype(BF16)
        dkv_ref[:, cols] = jnp.where(low, dks[0], dks[1]).astype(BF16)
        dkv_ref[:, vcols] = jnp.where(low, dvs[0], dvs[1]).astype(BF16)
    half = events // 2
    core = core_ref[0]
    mine = pl.ds(pl.multiple_of(core * half, half), half)
    other = pl.ds(pl.multiple_of((1 - core) * half, half), half)
    other_ref[...] = nt(dkv_ref[other, :], kvw_ref[...]).astype(BF16)
    mine_ref[...] = nt(dkv_ref[mine, :], kvw_ref[...])


def add_kernel(one_ref, two_ref, *rest):
    rest[-1][...] = (one_ref[...].astype(F32) + two_ref[...].astype(F32)).astype(BF16)


def halves_kernel(core_ref, mine_ref, other_ref, out_hbm, sems):
    half = mine_ref.shape[0]
    core = core_ref[0]
    mine = out_hbm.at[pl.ds(pl.multiple_of(core * half, half), half)]
    other = out_hbm.at[pl.ds(pl.multiple_of((1 - core) * half, half), half)]
    for copy in start(sems, (mine_ref, mine), (other_ref, other)):
        copy.wait()


def final_kernel(part_ref, base_ref, weight_ref, result_ref):
    own, width = base_ref.shape
    parts = part_ref.shape[0] // own
    dq = jnp.sum(part_ref[...].astype(F32).reshape(parts, own, width), axis=0) * 0.0625
    result_ref[...] = (base_ref[...] + nt(dq.astype(BF16), weight_ref[...])).astype(BF16)


def shards(
    history_embed,
    candidate_embed,
    query_weight,
    unit_weight,
    keyval_weight,
    output_weight,
    block_user,
    block_length,
    candidate_user,
    grad_output,
):
    own, width = candidate_embed.shape
    events = history_embed.shape[0]
    plane = lax.axis_size("plane")
    column = own * HIGH
    rows = column * plane
    s = jax.ShapeDtypeStruct

    def from_up(value, k):
        return lax.ppermute(value, "high", [((i + k) % HIGH, i) for i in range(HIGH)])

    def exchange(value):
        parts = value.reshape(plane, column, value.shape[-1])
        return lax.all_to_all(parts, "plane", 0, 0).reshape(rows, value.shape[-1])

    high = lax.axis_index("high").reshape(1)
    sems = pltpu.SemaphoreType.DMA
    full = width + LANES + width
    pack = call(
        pack_kernel,
        "hhh",
        [(s((own, full), BF16), "v")],
        [pltpu.VMEM((1, own), jnp.int32), pltpu.VMEM((own, width), BF16), pltpu.VMEM((own, width), BF16), sems((3,))],
        limit=WHOLE,
    )(candidate_user.reshape(1, own), candidate_embed, grad_output)[0]
    wide = (s((PAIRS, 2 * events, LANES), BF16), "v")
    keys, values = call(keyval_kernel, "svv", [wide, wide], flops=1 << 30)(
        block_length, history_embed, keyval_weight
    )
    core = (lax.axis_index("cand") & 1).reshape(1)
    pay, spread = call(
        spread_kernel,
        "svvvvhss",
        [(s((column, full), BF16), "v"), (s((plane, column, width + LANES), BF16), "v")],
    )(high, pack, *[from_up(pack, k) for k in (1, 2, 3)], keys, block_user, core)
    pay_all = exchange(spread)

    col_f32 = (s((column, width), F32), "v")
    col_b16 = (s((column, width), BF16), "v")
    own_f32 = (s((own, width), F32), "v")
    own_b16 = (s((own, width), BF16), "v")
    big = (s((rows, width), BF16), "v")
    gate, uslope, dgated = call(own_kernel, "vvv", [col_f32] * 3, flops=1 << 26)(
        pay, unit_weight, output_weight
    )
    query, att = call(forward_kernel, "svvvv", [big, big], flops=1 << 31)(
        block_user, pay_all, query_weight, keys, values
    )
    att_all = exchange(att)
    att_col = call(sum_kernel, "v", [col_b16], flops=1 << 20)(att_all)[0]
    datt, gated, dunit = call(
        norm_kernel, "s" + "v" * 7, [(s((plane, column, width), BF16), "v"), own_b16, own_b16], flops=1 << 20
    )(high, att_col, *[from_up(att_col, k) for k in (1, 2, 3)], gate, dgated, uslope)
    datt_all = exchange(datt)
    candidate_output, base = call(output_kernel, "v" * 6, [own_b16, own_f32], flops=1 << 26)(
        candidate_embed, grad_output, gated, dunit, output_weight, unit_weight
    )
    half = events // 2
    half_b16 = (s((half, width), BF16), "v")
    dq, mine, other = call(
        backward_kernel,
        "ssvvvvvv",
        [big, (s((half, width), F32), "v"), half_b16],
        [pltpu.VMEM((rows, width), BF16), pltpu.VMEM((events, 2 * width), BF16)],
        flops=1 << 32,
    )(block_user, core, pay_all, query, datt_all, keys, values, keyval_weight)
    dq_all = lax.all_to_all(
        dq.reshape(plane * HIGH, own, width), ("plane", "high"), 0, 0
    ).reshape(rows, width)
    swap_core = [(i, i ^ 1) for i in range(4)]
    swap_chip = [(i, i ^ 2) for i in range(4)]
    got = lax.ppermute(other, "cand", swap_core)
    pair = call(add_kernel, "vv", [half_b16])(mine, got)[0]
    got = lax.ppermute(pair, "cand", swap_chip)
    quad = call(add_kernel, "vv", [half_b16])(pair, got)[0]
    got = lax.ppermute(quad, "cand", swap_core)
    history_grad = call(halves_kernel, "svv", [(s((events, width), BF16), "h")], [sems((2,))])(
        core, quad, got
    )[0]
    candidate_grad = call(final_kernel, "v" * 3, [own_b16], flops=1 << 26)(dq_all, base, query_weight)[0]
    return (candidate_output, history_grad, candidate_grad)


def solution(mesh):
    seq, cand = mesh.shape["seq"], mesh.shape["cand"]
    fine = Mesh(mesh.devices.reshape(seq // HIGH, HIGH, cand), ("plane", "high", "cand"))
    hist, full = ("plane", "high"), ("plane", "high", "cand")
    in_specs = (
        P(hist, None),
        P(full, None),
        P(),
        P(),
        P(),
        P(),
        P(hist),
        P(hist),
        P(full),
        P(full, None),
    )
    out_specs = (P(full, None), P(hist, None), P(full, None))
    return jax.shard_map(shards, mesh=fine, in_specs=in_specs, out_specs=out_specs, check_vma=False)
```

```python
import jax
import jax.numpy as jnp
from jax import lax
from jax.experimental import pallas as pl
from jax.experimental.pallas import tpu as pltpu
from jax.sharding import Mesh, PartitionSpec as P

HEADS = 8
PAIRS = 4
LANES = 128
F32 = jnp.float32
BF16 = jnp.bfloat16
SMALL = 16 * 1024 * 1024
HIGH = 4
STEP = 256


def nn(a, b):
    return lax.dot_general(a, b, (((1,), (0,)), ((), ())), preferred_element_type=F32)


def nt(a, b):
    return lax.dot_general(a, b, (((1,), (1,)), ((), ())), preferred_element_type=F32)


def call(body, ins, outs, scratch=(), flops=0, limit=SMALL):
    place = {"v": pltpu.VMEM, "s": pltpu.SMEM, "h": pltpu.HBM, "a": pl.ANY}
    spec = [pl.BlockSpec(memory_space=place[i]) for i in ins]
    shapes = [shape for shape, _ in outs]
    out_spec = [pl.BlockSpec(memory_space=place[i]) for _, i in outs]
    return pl.pallas_call(
        body,
        out_shape=shapes,
        in_specs=spec,
        out_specs=out_spec,
        scratch_shapes=list(scratch),
        compiler_params=pltpu.CompilerParams(vmem_limit_bytes=limit),
        cost_estimate=pl.CostEstimate(flops=flops, bytes_accessed=1 << 20, transcendentals=0),
    )


def start(sems, *pairs):
    copies = [pltpu.make_async_copy(src, dst, sems.at[i]) for i, (src, dst) in enumerate(pairs)]
    for copy in copies:
        copy.start()
    return copies


def touch_kernel(ref, out_ref):
    out_ref[...] = ref[:16, :LANES]


def spread_kernel(high_ref, own_ref, one_ref, two_ref, three_ref, *rest):
    column_ref, plane_ref = rest[-2:]
    refs = (own_ref, one_ref, two_ref, three_ref)
    column = jnp.concatenate([r[...].astype(F32) for r in refs], axis=0)
    column = pltpu.roll(column, high_ref[0] * own_ref.shape[0], 0).astype(BF16)
    column_ref[...] = column
    for i in range(plane_ref.shape[0]):
        plane_ref[i] = column[:, : plane_ref.shape[2]]


def put_keyval(length, hist_ref, weight_ref, key_ref, value_ref):
    events = hist_ref.shape[0]
    keyval = nn(hist_ref[...], weight_ref[...])
    row = lax.broadcasted_iota(jnp.int32, (events, LANES), 0)
    lane = lax.broadcasted_iota(jnp.int32, (events, LANES), 1)
    live = row < length
    half = LANES // 2
    for p in range(PAIRS):
        for ref, base in ((key_ref, 0), (value_ref, PAIRS * LANES)):
            part = keyval[:, base + p * LANES : base + (p + 1) * LANES]
            ref[p, :events, :] = jnp.where(live & (lane < half), part, 0.0).astype(BF16)
            ref[p, events:, :] = jnp.where(live & (lane >= half), part, 0.0).astype(BF16)


def forward_kernel(
    user_ref, length_ref, pay_ref, weight_ref, hist_ref, kvw_ref, key_ref, value_ref, query_ref, att_ref
):
    rows, width = query_ref.shape
    put_keyval(length_ref[0], hist_ref, kvw_ref, key_ref, value_ref)
    pay = pay_ref[...]
    mine = pay[:, width : width + 1].astype(F32) == user_ref[0].astype(F32)
    query = nn(pay[:, :width], weight_ref[...]).astype(BF16).astype(F32)
    query_ref[...] = jnp.where(mine, query * 0.0625, 0.0).astype(BF16)
    for p in range(PAIRS):
        cols = slice(p * LANES, (p + 1) * LANES)
        for r in range(0, rows, STEP):
            r = slice(r, r + STEP)
            u = nt(query_ref[r, cols], key_ref[p])
            w = (u + u * jnp.tanh(u)).astype(BF16)
            att_ref[r, cols] = nn(w, value_ref[p]).astype(BF16)


def own_kernel(pay_ref, unit_ref, out_ref, gate_ref, uslope_ref, dgated_ref):
    width = unit_ref.shape[0]
    pay = pay_ref[...]
    linear = nn(pay[:, :width], unit_ref[...])
    sig = jax.nn.sigmoid(linear)
    gate_ref[...] = (linear * sig).astype(BF16).astype(F32)
    uslope_ref[...] = sig * (1.0 + linear * (1.0 - sig))
    dgated_ref[...] = nt(pay[:, width + LANES :], out_ref[...])


def sum_kernel(part_ref, out_ref):
    own, width = out_ref.shape
    parts = part_ref.shape[0] // own
    total = jnp.sum(part_ref[...].astype(F32).reshape(parts, own, width), axis=0)
    out_ref[...] = total.astype(out_ref.dtype)


def norm_kernel(
    high_ref, own_ref, one_ref, two_ref, three_ref, gate_ref, dgated_ref, uslope_ref, datt_ref, gated_ref, dunit_ref
):
    own, width = gate_ref.shape
    block = own // HIGH
    refs = (own_ref, one_ref, two_ref, three_ref)
    att = sum(ref[...].astype(F32) for ref in refs)
    mean = jnp.mean(att, axis=1, keepdims=True)
    centered = att - mean
    inverse = lax.rsqrt(jnp.mean(centered * centered, axis=1, keepdims=True) + 1e-05)
    normed = centered * inverse
    gate = gate_ref[...]
    dgated = dgated_ref[...]
    g = dgated * gate
    datt = inverse * (
        g
        - jnp.mean(g, axis=1, keepdims=True)
        - normed * jnp.mean(g * normed, axis=1, keepdims=True)
    )
    datt = datt.astype(BF16)
    for i in range(datt_ref.shape[0]):
        datt_ref[i] = datt
    down = ((HIGH - high_ref[0]) & (HIGH - 1)) * block
    gated_ref[...] = pltpu.roll(normed * gate, down, 0)[:block].astype(BF16)
    dunit_ref[...] = pltpu.roll(dgated * normed * uslope_ref[...], down, 0)[:block].astype(BF16)


def output_kernel(embed_ref, grad_ref, gated_ref, dunit_ref, out_ref, unit_ref, result_ref, base_ref):
    result_ref[...] = (embed_ref[...].astype(F32) + nn(gated_ref[...], out_ref[...])).astype(BF16)
    base_ref[...] = grad_ref[...].astype(F32) + nt(dunit_ref[...], unit_ref[...])


def silu_pair(u):
    t = jnp.tanh(u)
    ut = u * t
    return u + ut, (1.0 + t) + (u - ut * t)


def backward_kernel(
    user_ref, core_ref, pay_ref, query_ref, datt_ref, key_ref, value_ref, kvw_ref,
    dq_ref, mine_ref, other_ref, masked_ref, dkv_ref,
):
    width = datt_ref.shape[1]
    events = value_ref.shape[1] // 2
    owned = pay_ref[...][:, width : width + 1].astype(F32) == user_ref[0].astype(F32)
    masked_ref[...] = jnp.where(owned, datt_ref[...].astype(F32), 0.0).astype(BF16)
    low = lax.broadcasted_iota(jnp.int32, (events, LANES), 1) < LANES // 2
    for p in range(PAIRS):
        cols = slice(p * LANES, (p + 1) * LANES)
        vcols = slice(width + p * LANES, width + (p + 1) * LANES)
        datt = masked_ref[:, cols]
        query = query_ref[:, cols]
        dks, dvs, dqs = [], [], []
        for r in (slice(0, events), slice(events, 2 * events)):
            key = key_ref[p, r, :]
            weight, slope = silu_pair(nt(key, query))
            ds = (nt(value_ref[p, r, :], datt) * slope).astype(BF16)
            dks.append(nn(ds, query))
            dvs.append(nn(weight.astype(BF16), datt))
            dqs.append(nn(key.T, ds))
        dq_ref[:, cols] = (dqs[0] + dqs[1]).T.astype(BF16)
        dkv_ref[:, cols] = jnp.where(low, dks[0], dks[1]).astype(BF16)
        dkv_ref[:, vcols] = jnp.where(low, dvs[0], dvs[1]).astype(BF16)
    half = events // 2
    core = core_ref[0]
    mine = pl.ds(pl.multiple_of(core * half, half), half)
    other = pl.ds(pl.multiple_of((1 - core) * half, half), half)
    other_ref[...] = nt(dkv_ref[other, :], kvw_ref[...]).astype(BF16)
    mine_ref[...] = nt(dkv_ref[mine, :], kvw_ref[...])


def add_kernel(one_ref, two_ref, *rest):
    rest[-1][...] = (one_ref[...].astype(F32) + two_ref[...].astype(F32)).astype(BF16)


def halves_kernel(core_ref, mine_ref, other_ref, out_hbm, sems):
    half = mine_ref.shape[0]
    core = core_ref[0]
    mine = out_hbm.at[pl.ds(pl.multiple_of(core * half, half), half)]
    other = out_hbm.at[pl.ds(pl.multiple_of((1 - core) * half, half), half)]
    for copy in start(sems, (mine_ref, mine), (other_ref, other)):
        copy.wait()


def final_kernel(part_ref, base_ref, weight_ref, result_ref):
    own, width = base_ref.shape
    parts = part_ref.shape[0] // own
    dq = jnp.sum(part_ref[...].astype(F32).reshape(parts, own, width), axis=0) * 0.0625
    result_ref[...] = (base_ref[...] + nt(dq.astype(BF16), weight_ref[...])).astype(BF16)


def shards(
    history_embed,
    candidate_embed,
    query_weight,
    unit_weight,
    keyval_weight,
    output_weight,
    block_user,
    block_length,
    candidate_user,
    grad_output,
):
    own, width = candidate_embed.shape
    events = history_embed.shape[0]
    plane = lax.axis_size("plane")
    column = own * HIGH
    rows = column * plane
    s = jax.ShapeDtypeStruct

    def from_up(value, k):
        return lax.ppermute(value, "high", [((i + k) % HIGH, i) for i in range(HIGH)])

    def exchange(value):
        parts = value.reshape(plane, column, value.shape[-1])
        return lax.all_to_all(parts, "plane", 0, 0).reshape(rows, value.shape[-1])

    high = lax.axis_index("high").reshape(1)
    sems = pltpu.SemaphoreType.DMA
    full = width + LANES + width
    user = jnp.broadcast_to(candidate_user[:, None], (own, LANES)).astype(BF16)
    pack = jnp.concatenate([candidate_embed, user, grad_output], axis=1)
    wide = (s((PAIRS, 2 * events, LANES), BF16), "v")
    core = (lax.axis_index("cand") & 1).reshape(1)
    touched = call(touch_kernel, "v", [(s((16, LANES), BF16), "v")])(keyval_weight)[0]
    pay, spread = call(
        spread_kernel,
        "svvvvsssa",
        [(s((column, full), BF16), "v"), (s((plane, column, width + LANES), BF16), "v")],
    )(high, pack, *[from_up(pack, k) for k in (1, 2, 3)], block_user, block_length, core, touched)
    pay_all = exchange(spread)

    col_f32 = (s((column, width), F32), "v")
    col_b16 = (s((column, width), BF16), "v")
    own_f32 = (s((own, width), F32), "v")
    own_b16 = (s((own, width), BF16), "v")
    big = (s((rows, width), BF16), "v")
    gate, uslope, dgated = call(own_kernel, "vvv", [col_f32] * 3, flops=1 << 26)(
        pay, unit_weight, output_weight
    )
    keys, values, query, att = call(forward_kernel, "ssvvvv", [wide, wide, big, big], flops=1 << 31)(
        block_user, block_length, pay_all, query_weight, history_embed, keyval_weight
    )
    att_all = exchange(att)
    att_col = call(sum_kernel, "v", [col_b16], flops=1 << 20)(att_all)[0]
    datt, gated, dunit = call(
        norm_kernel, "s" + "v" * 7, [(s((plane, column, width), BF16), "v"), own_b16, own_b16], flops=1 << 20
    )(high, att_col, *[from_up(att_col, k) for k in (1, 2, 3)], gate, dgated, uslope)
    datt_all = exchange(datt)
    candidate_output, base = call(output_kernel, "v" * 6, [own_b16, own_f32], flops=1 << 26)(
        candidate_embed, grad_output, gated, dunit, output_weight, unit_weight
    )
    half = events // 2
    half_b16 = (s((half, width), BF16), "v")
    dq, mine, other = call(
        backward_kernel,
        "ssvvvvvv",
        [big, (s((half, width), F32), "v"), half_b16],
        [pltpu.VMEM((rows, width), BF16), pltpu.VMEM((events, 2 * width), BF16)],
        flops=1 << 32,
    )(block_user, core, pay_all, query, datt_all, keys, values, keyval_weight)
    dq_all = lax.all_to_all(
        dq.reshape(plane * HIGH, own, width), ("plane", "high"), 0, 0
    ).reshape(rows, width)
    swap_core = [(i, i ^ 1) for i in range(4)]
    swap_chip = [(i, i ^ 2) for i in range(4)]
    got = lax.ppermute(other, "cand", swap_core)
    pair = call(add_kernel, "vv", [half_b16])(mine, got)[0]
    got = lax.ppermute(pair, "cand", swap_chip)
    quad = call(add_kernel, "vv", [half_b16])(pair, got)[0]
    got = lax.ppermute(quad, "cand", swap_core)
    history_grad = call(halves_kernel, "svv", [(s((events, width), BF16), "h")], [sems((2,))])(
        core, quad, got
    )[0]
    candidate_grad = call(final_kernel, "v" * 3, [own_b16], flops=1 << 26)(dq_all, base, query_weight)[0]
    return (candidate_output, history_grad, candidate_grad)


def solution(mesh):
    seq, cand = mesh.shape["seq"], mesh.shape["cand"]
    fine = Mesh(mesh.devices.reshape(seq // HIGH, HIGH, cand), ("plane", "high", "cand"))
    hist, full = ("plane", "high"), ("plane", "high", "cand")
    in_specs = (
        P(hist, None),
        P(full, None),
        P(),
        P(),
        P(),
        P(),
        P(hist),
        P(hist),
        P(full),
        P(full, None),
    )
    out_specs = (P(full, None), P(hist, None), P(full, None))
    return jax.shard_map(shards, mesh=fine, in_specs=in_specs, out_specs=out_specs, check_vma=False)
```

```python
import jax
import jax.numpy as jnp
from jax import lax
from jax.experimental import pallas as pl
from jax.experimental.pallas import tpu as pltpu
from jax.sharding import Mesh, PartitionSpec as P

HEADS = 8
PAIRS = 4
LANES = 128
F32 = jnp.float32
BF16 = jnp.bfloat16
EARLY = 2
SMALL = 10 * 1024 * 1024
HIGH = 4
STEP = 256


def nn(a, b):
    return lax.dot_general(a, b, (((1,), (0,)), ((), ())), preferred_element_type=F32)


def nt(a, b):
    return lax.dot_general(a, b, (((1,), (1,)), ((), ())), preferred_element_type=F32)


def call(body, ins, outs, scratch=(), flops=0, limit=SMALL):
    place = {"v": pltpu.VMEM, "s": pltpu.SMEM, "h": pltpu.HBM, "a": pl.ANY}
    spec = [pl.BlockSpec(memory_space=place[i]) for i in ins]
    shapes = [shape for shape, _ in outs]
    out_spec = [pl.BlockSpec(memory_space=place[i]) for _, i in outs]
    return pl.pallas_call(
        body,
        out_shape=shapes,
        in_specs=spec,
        out_specs=out_spec,
        scratch_shapes=list(scratch),
        compiler_params=pltpu.CompilerParams(vmem_limit_bytes=limit),
        cost_estimate=pl.CostEstimate(flops=flops, bytes_accessed=1 << 20, transcendentals=0),
    )


def start(sems, *pairs):
    copies = [pltpu.make_async_copy(src, dst, sems.at[i]) for i, (src, dst) in enumerate(pairs)]
    for copy in copies:
        copy.start()
    return copies


def touch_kernel(ref, out_ref):
    out_ref[...] = ref[:16, :LANES]


def spread_kernel(high_ref, own_ref, one_ref, two_ref, three_ref, *rest):
    column_ref, plane_ref = rest[-2:]
    refs = (own_ref, one_ref, two_ref, three_ref)
    column = jnp.concatenate([r[...].astype(F32) for r in refs], axis=0)
    column = pltpu.roll(column, high_ref[0] * own_ref.shape[0], 0).astype(BF16)
    column_ref[...] = column
    for i in range(plane_ref.shape[0]):
        plane_ref[i] = column[:, : plane_ref.shape[2]]


def put_keyval(length, hist_ref, weight_ref, key_ref, value_ref):
    events = hist_ref.shape[0]
    keyval = nn(hist_ref[...], weight_ref[...])
    row = lax.broadcasted_iota(jnp.int32, (events, LANES), 0)
    lane = lax.broadcasted_iota(jnp.int32, (events, LANES), 1)
    live = row < length
    half = LANES // 2
    for p in range(PAIRS):
        for ref, base in ((key_ref, 0), (value_ref, PAIRS * LANES)):
            part = keyval[:, base + p * LANES : base + (p + 1) * LANES]
            ref[p, :events, :] = jnp.where(live & (lane < half), part, 0.0).astype(BF16)
            ref[p, events:, :] = jnp.where(live & (lane >= half), part, 0.0).astype(BF16)


def forward_kernel(
    user_ref, length_ref, pay_ref, weight_ref, hist_ref, kvw_ref, key_ref, value_ref, query_ref, att_ref
):
    rows, width = query_ref.shape
    put_keyval(length_ref[0], hist_ref, kvw_ref, key_ref, value_ref)
    pay = pay_ref[...]
    mine = pay[:, width : width + 1].astype(F32) == user_ref[0].astype(F32)
    query = nn(pay[:, :width], weight_ref[...]).astype(BF16).astype(F32)
    query_ref[...] = jnp.where(mine, query * 0.0625, 0.0).astype(BF16)
    for p in range(PAIRS):
        cols = slice(p * LANES, (p + 1) * LANES)
        for r in range(0, rows, STEP):
            r = slice(r, r + STEP)
            u = nt(query_ref[r, cols], key_ref[p])
            w = (u + u * jnp.tanh(u)).astype(BF16)
            att_ref[r, cols] = nn(w, value_ref[p]).astype(BF16)


def own_kernel(pay_ref, unit_ref, out_ref, gate_ref, uslope_ref, dgated_ref):
    width = unit_ref.shape[0]
    pay = pay_ref[...]
    linear = nn(pay[:, :width], unit_ref[...])
    sig = jax.nn.sigmoid(linear)
    gate_ref[...] = (linear * sig).astype(BF16).astype(F32)
    uslope_ref[...] = sig * (1.0 + linear * (1.0 - sig))
    dgated_ref[...] = nt(pay[:, width + LANES :], out_ref[...])


def sum_kernel(part_ref, out_ref):
    own, width = out_ref.shape
    parts = part_ref.shape[0] // own
    total = jnp.sum(part_ref[...].astype(F32).reshape(parts, own, width), axis=0)
    out_ref[...] = total.astype(out_ref.dtype)


def norm_kernel(
    high_ref, own_ref, one_ref, two_ref, three_ref, gate_ref, dgated_ref, uslope_ref, _, datt_ref, gated_ref, dunit_ref
):
    own, width = gate_ref.shape
    block = own // HIGH
    refs = (own_ref, one_ref, two_ref, three_ref)
    att = sum(ref[...].astype(F32) for ref in refs)
    mean = jnp.mean(att, axis=1, keepdims=True)
    centered = att - mean
    inverse = lax.rsqrt(jnp.mean(centered * centered, axis=1, keepdims=True) + 1e-05)
    normed = centered * inverse
    gate = gate_ref[...]
    dgated = dgated_ref[...]
    g = dgated * gate
    datt = inverse * (
        g
        - jnp.mean(g, axis=1, keepdims=True)
        - normed * jnp.mean(g * normed, axis=1, keepdims=True)
    )
    datt = datt.astype(BF16)
    for i in range(datt_ref.shape[0]):
        datt_ref[i] = datt
    down = ((HIGH - high_ref[0]) & (HIGH - 1)) * block
    gated_ref[...] = pltpu.roll(normed * gate, down, 0)[:block].astype(BF16)
    dunit_ref[...] = pltpu.roll(dgated * normed * uslope_ref[...], down, 0)[:block].astype(BF16)


def output_kernel(embed_ref, grad_ref, gated_ref, dunit_ref, out_ref, unit_ref, result_ref, base_ref):
    result_ref[...] = (embed_ref[...].astype(F32) + nn(gated_ref[...], out_ref[...])).astype(BF16)
    base_ref[...] = grad_ref[...].astype(F32) + nt(dunit_ref[...], unit_ref[...])


def silu_pair(u):
    t = jnp.tanh(u)
    ut = u * t
    return u + ut, (1.0 + t) + (u - ut * t)


def early_kernel(query_ref, key_ref, weight_ref, slope_ref):
    events = key_ref.shape[1] // 2
    for p in range(EARLY):
        cols = slice(p * LANES, (p + 1) * LANES)
        for r in (slice(0, events), slice(events, 2 * events)):
            weight, slope = silu_pair(nt(key_ref[p, r, :], query_ref[:, cols]))
            weight_ref[p, r, :] = weight.astype(BF16)
            slope_ref[p, r, :] = slope.astype(BF16)


def backward_kernel(
    user_ref, core_ref, pay_ref, query_ref, datt_ref, key_ref, value_ref, kvw_ref, weight_ref, slope_ref,
    dq_ref, mine_ref, other_ref, masked_ref, dkv_ref,
):
    width = datt_ref.shape[1]
    events = value_ref.shape[1] // 2
    owned = pay_ref[...][:, width : width + 1].astype(F32) == user_ref[0].astype(F32)
    masked_ref[...] = jnp.where(owned, datt_ref[...].astype(F32), 0.0).astype(BF16)
    low = lax.broadcasted_iota(jnp.int32, (events, LANES), 1) < LANES // 2
    for p in range(PAIRS):
        cols = slice(p * LANES, (p + 1) * LANES)
        vcols = slice(width + p * LANES, width + (p + 1) * LANES)
        datt = masked_ref[:, cols]
        query = query_ref[:, cols]
        dks, dvs, dqs = [], [], []
        for r in (slice(0, events), slice(events, 2 * events)):
            key = key_ref[p, r, :]
            if p < EARLY:
                weight, slope = weight_ref[p, r, :], slope_ref[p, r, :].astype(F32)
            else:
                weight, slope = silu_pair(nt(key, query))
            ds = (nt(value_ref[p, r, :], datt) * slope).astype(BF16)
            dks.append(nn(ds, query))
            dvs.append(nn(weight.astype(BF16), datt))
            dqs.append(nn(key.T, ds))
        dq_ref[:, cols] = (dqs[0] + dqs[1]).T.astype(BF16)
        dkv_ref[:, cols] = jnp.where(low, dks[0], dks[1]).astype(BF16)
        dkv_ref[:, vcols] = jnp.where(low, dvs[0], dvs[1]).astype(BF16)
    half = events // 2
    core = core_ref[0]
    mine = pl.ds(pl.multiple_of(core * half, half), half)
    other = pl.ds(pl.multiple_of((1 - core) * half, half), half)
    other_ref[...] = nt(dkv_ref[other, :], kvw_ref[...]).astype(BF16)
    mine_ref[...] = nt(dkv_ref[mine, :], kvw_ref[...])


def add_kernel(one_ref, two_ref, *rest):
    rest[-1][...] = (one_ref[...].astype(F32) + two_ref[...].astype(F32)).astype(BF16)


def halves_kernel(core_ref, mine_ref, other_ref, out_hbm, sems):
    half = mine_ref.shape[0]
    core = core_ref[0]
    mine = out_hbm.at[pl.ds(pl.multiple_of(core * half, half), half)]
    other = out_hbm.at[pl.ds(pl.multiple_of((1 - core) * half, half), half)]
    for copy in start(sems, (mine_ref, mine), (other_ref, other)):
        copy.wait()


def final_kernel(part_ref, base_ref, weight_ref, result_ref):
    own, width = base_ref.shape
    parts = part_ref.shape[0] // own
    dq = jnp.sum(part_ref[...].astype(F32).reshape(parts, own, width), axis=0) * 0.0625
    result_ref[...] = (base_ref[...] + nt(dq.astype(BF16), weight_ref[...])).astype(BF16)


def shards(
    history_embed,
    candidate_embed,
    query_weight,
    unit_weight,
    keyval_weight,
    output_weight,
    block_user,
    block_length,
    candidate_user,
    grad_output,
):
    own, width = candidate_embed.shape
    events = history_embed.shape[0]
    plane = lax.axis_size("plane")
    column = own * HIGH
    rows = column * plane
    s = jax.ShapeDtypeStruct

    def from_up(value, k):
        return lax.ppermute(value, "high", [((i + k) % HIGH, i) for i in range(HIGH)])

    def exchange(value):
        parts = value.reshape(plane, column, value.shape[-1])
        return lax.all_to_all(parts, "plane", 0, 0).reshape(rows, value.shape[-1])

    high = lax.axis_index("high").reshape(1)
    sems = pltpu.SemaphoreType.DMA
    full = width + LANES + width
    user = jnp.broadcast_to(candidate_user[:, None], (own, LANES)).astype(BF16)
    pack = jnp.concatenate([candidate_embed, user, grad_output], axis=1)
    wide = (s((PAIRS, 2 * events, LANES), BF16), "v")
    core = (lax.axis_index("cand") & 1).reshape(1)
    touched = call(touch_kernel, "v", [(s((16, LANES), BF16), "v")])(keyval_weight)[0]
    pay, spread = call(
        spread_kernel,
        "svvvvsssa",
        [(s((column, full), BF16), "v"), (s((plane, column, width + LANES), BF16), "v")],
    )(high, pack, *[from_up(pack, k) for k in (1, 2, 3)], block_user, block_length, core, touched)
    pay_all = exchange(spread)

    col_f32 = (s((column, width), F32), "v")
    col_b16 = (s((column, width), BF16), "v")
    own_f32 = (s((own, width), F32), "v")
    own_b16 = (s((own, width), BF16), "v")
    big = (s((rows, width), BF16), "v")
    gate, uslope, dgated = call(own_kernel, "vvv", [col_f32] * 3, flops=1 << 26)(
        pay, unit_weight, output_weight
    )
    keys, values, query, att = call(forward_kernel, "ssvvvv", [wide, wide, big, big], flops=1 << 31)(
        block_user, block_length, pay_all, query_weight, history_embed, keyval_weight
    )
    att_all = exchange(att)
    early = (s((EARLY, 2 * events, rows), BF16), "v")
    weight, slope = call(early_kernel, "vv", [early, early], flops=1 << 28)(query, keys)
    att_col = call(sum_kernel, "v", [col_b16], flops=1 << 20)(att_all)[0]
    datt, gated, dunit = call(
        norm_kernel, "s" + "v" * 7 + "a", [(s((plane, column, width), BF16), "v"), own_b16, own_b16], flops=1 << 20
    )(high, att_col, *[from_up(att_col, k) for k in (1, 2, 3)], gate, dgated, uslope, weight)
    datt_all = exchange(datt)
    candidate_output, base = call(output_kernel, "v" * 6, [own_b16, own_f32], flops=1 << 26)(
        candidate_embed, grad_output, gated, dunit, output_weight, unit_weight
    )
    half = events // 2
    half_b16 = (s((half, width), BF16), "v")
    dq, mine, other = call(
        backward_kernel,
        "ssvvvvvvvv",
        [big, (s((half, width), F32), "v"), half_b16],
        [pltpu.VMEM((rows, width), BF16), pltpu.VMEM((events, 2 * width), BF16)],
        flops=1 << 32,
    )(block_user, core, pay_all, query, datt_all, keys, values, keyval_weight, weight, slope)
    dq_all = lax.all_to_all(
        dq.reshape(plane * HIGH, own, width), ("plane", "high"), 0, 0
    ).reshape(rows, width)
    swap_core = [(i, i ^ 1) for i in range(4)]
    swap_chip = [(i, i ^ 2) for i in range(4)]
    got = lax.ppermute(other, "cand", swap_core)
    pair = call(add_kernel, "vv", [half_b16])(mine, got)[0]
    got = lax.ppermute(pair, "cand", swap_chip)
    quad = call(add_kernel, "vv", [half_b16])(pair, got)[0]
    got = lax.ppermute(quad, "cand", swap_core)
    history_grad = call(halves_kernel, "svv", [(s((events, width), BF16), "h")], [sems((2,))])(
        core, quad, got
    )[0]
    candidate_grad = call(final_kernel, "v" * 3, [own_b16], flops=1 << 26)(dq_all, base, query_weight)[0]
    return (candidate_output, history_grad, candidate_grad)


def solution(mesh):
    seq, cand = mesh.shape["seq"], mesh.shape["cand"]
    fine = Mesh(mesh.devices.reshape(seq // HIGH, HIGH, cand), ("plane", "high", "cand"))
    hist, full = ("plane", "high"), ("plane", "high", "cand")
    in_specs = (
        P(hist, None),
        P(full, None),
        P(),
        P(),
        P(),
        P(),
        P(hist),
        P(hist),
        P(full),
        P(full, None),
    )
    out_specs = (P(full, None), P(hist, None), P(full, None))
    return jax.shard_map(shards, mesh=fine, in_specs=in_specs, out_specs=out_specs, check_vma=False)
```

```python
import jax
import jax.numpy as jnp
from jax import lax
from jax.experimental import pallas as pl
from jax.experimental.pallas import tpu as pltpu
from jax.sharding import Mesh, PartitionSpec as P

HEADS = 8
PAIRS = 4
LANES = 128
F32 = jnp.float32
BF16 = jnp.bfloat16
EARLY = 2
SMALL = 10 * 1024 * 1024
HIGH = 4
STEP = 256


def nn(a, b):
    return lax.dot_general(a, b, (((1,), (0,)), ((), ())), preferred_element_type=F32)


def nt(a, b):
    return lax.dot_general(a, b, (((1,), (1,)), ((), ())), preferred_element_type=F32)


def call(body, ins, outs, scratch=(), flops=0, limit=SMALL):
    place = {"v": pltpu.VMEM, "s": pltpu.SMEM, "h": pltpu.HBM, "a": pl.ANY}
    spec = [pl.BlockSpec(memory_space=place[i]) for i in ins]
    shapes = [shape for shape, _ in outs]
    out_spec = [pl.BlockSpec(memory_space=place[i]) for _, i in outs]
    return pl.pallas_call(
        body,
        out_shape=shapes,
        in_specs=spec,
        out_specs=out_spec,
        scratch_shapes=list(scratch),
        compiler_params=pltpu.CompilerParams(vmem_limit_bytes=limit),
        cost_estimate=pl.CostEstimate(flops=flops, bytes_accessed=1 << 20, transcendentals=0),
    )


def start(sems, *pairs):
    copies = [pltpu.make_async_copy(src, dst, sems.at[i]) for i, (src, dst) in enumerate(pairs)]
    for copy in copies:
        copy.start()
    return copies


def touch_kernel(ref, out_ref):
    out_ref[...] = ref[:16, :LANES]


def spread_kernel(high_ref, own_ref, one_ref, two_ref, three_ref, *rest):
    column_ref, plane_ref = rest[-2:]
    refs = (own_ref, one_ref, two_ref, three_ref)
    column = jnp.concatenate([r[...].astype(F32) for r in refs], axis=0)
    column = pltpu.roll(column, high_ref[0] * own_ref.shape[0], 0).astype(BF16)
    column_ref[...] = column
    for i in range(plane_ref.shape[0]):
        plane_ref[i] = column[:, : plane_ref.shape[2]]


def put_keyval(length, hist_ref, weight_ref, key_ref, value_ref):
    events = hist_ref.shape[0]
    keyval = nn(hist_ref[...], weight_ref[...])
    row = lax.broadcasted_iota(jnp.int32, (events, LANES), 0)
    lane = lax.broadcasted_iota(jnp.int32, (events, LANES), 1)
    live = row < length
    half = LANES // 2
    for p in range(PAIRS):
        for ref, base in ((key_ref, 0), (value_ref, PAIRS * LANES)):
            part = keyval[:, base + p * LANES : base + (p + 1) * LANES]
            ref[p, :events, :] = jnp.where(live & (lane < half), part, 0.0).astype(BF16)
            ref[p, events:, :] = jnp.where(live & (lane >= half), part, 0.0).astype(BF16)


def forward_kernel(
    user_ref, length_ref, pay_ref, weight_ref, hist_ref, kvw_ref, key_ref, value_ref, query_ref, att_ref
):
    rows, width = query_ref.shape
    put_keyval(length_ref[0], hist_ref, kvw_ref, key_ref, value_ref)
    pay = pay_ref[...]
    mine = pay[:, width : width + 1].astype(F32) == user_ref[0].astype(F32)
    query = nn(pay[:, :width], weight_ref[...]).astype(BF16).astype(F32)
    query_ref[...] = jnp.where(mine, query * 0.0625, 0.0).astype(BF16)
    for p in range(PAIRS):
        cols = slice(p * LANES, (p + 1) * LANES)
        for r in range(0, rows, STEP):
            r = slice(r, r + STEP)
            u = nt(query_ref[r, cols], key_ref[p])
            w = (u + u * jnp.tanh(u)).astype(BF16)
            att_ref[r, cols] = nn(w, value_ref[p]).astype(BF16)


def own_kernel(pay_ref, unit_ref, out_ref, gate_ref, uslope_ref, dgated_ref):
    width = unit_ref.shape[0]
    pay = pay_ref[...]
    linear = nn(pay[:, :width], unit_ref[...])
    sig = jax.nn.sigmoid(linear)
    gate_ref[...] = (linear * sig).astype(BF16).astype(F32)
    uslope_ref[...] = sig * (1.0 + linear * (1.0 - sig))
    dgated_ref[...] = nt(pay[:, width + LANES :], out_ref[...])


def sum_kernel(part_ref, out_ref):
    own, width = out_ref.shape
    parts = part_ref.shape[0] // own
    total = jnp.sum(part_ref[...].astype(F32).reshape(parts, own, width), axis=0)
    out_ref[...] = total.astype(out_ref.dtype)


def norm_kernel(
    high_ref, own_ref, one_ref, two_ref, three_ref, gate_ref, dgated_ref, uslope_ref, _, datt_ref, gated_ref, dunit_ref
):
    own, width = gate_ref.shape
    block = own // HIGH
    refs = (own_ref, one_ref, two_ref, three_ref)
    att = sum(ref[...].astype(F32) for ref in refs)
    mean = jnp.mean(att, axis=1, keepdims=True)
    centered = att - mean
    inverse = lax.rsqrt(jnp.mean(centered * centered, axis=1, keepdims=True) + 1e-05)
    normed = centered * inverse
    gate = gate_ref[...]
    dgated = dgated_ref[...]
    g = dgated * gate
    datt = inverse * (
        g
        - jnp.mean(g, axis=1, keepdims=True)
        - normed * jnp.mean(g * normed, axis=1, keepdims=True)
    )
    datt = datt.astype(BF16)
    for i in range(datt_ref.shape[0]):
        datt_ref[i] = datt
    down = ((HIGH - high_ref[0]) & (HIGH - 1)) * block
    gated_ref[...] = pltpu.roll(normed * gate, down, 0)[:block].astype(BF16)
    dunit_ref[...] = pltpu.roll(dgated * normed * uslope_ref[...], down, 0)[:block].astype(BF16)


def output_kernel(embed_ref, grad_ref, gated_ref, dunit_ref, out_ref, unit_ref, result_ref, base_ref):
    result_ref[...] = (embed_ref[...].astype(F32) + nn(gated_ref[...], out_ref[...])).astype(BF16)
    base_ref[...] = grad_ref[...].astype(F32) + nt(dunit_ref[...], unit_ref[...])


def silu_pair(u):
    t = jnp.tanh(u)
    ut = u * t
    return u + ut, (1.0 + t) + (u - ut * t)


def early_kernel(query_ref, key_ref, weight_ref, slope_ref):
    events = key_ref.shape[1] // 2
    for p in range(EARLY):
        cols = slice(p * LANES, (p + 1) * LANES)
        for r in (slice(0, events), slice(events, 2 * events)):
            weight, slope = silu_pair(nt(key_ref[p, r, :], query_ref[:, cols]))
            weight_ref[p, r, :] = weight.astype(BF16)
            slope_ref[p, r, :] = slope.astype(BF16)


def backward_kernel(
    user_ref, core_ref, pay_ref, query_ref, datt_ref, key_ref, value_ref, kvw_ref, weight_ref, slope_ref,
    dq_ref, mine_ref, other_ref, masked_ref, dkv_ref,
):
    width = datt_ref.shape[1]
    events = value_ref.shape[1] // 2
    owned = pay_ref[...][:, width : width + 1].astype(F32) == user_ref[0].astype(F32)
    masked_ref[...] = jnp.where(owned, datt_ref[...].astype(F32), 0.0).astype(BF16)
    low = lax.broadcasted_iota(jnp.int32, (events, LANES), 1) < LANES // 2
    for p in range(PAIRS):
        cols = slice(p * LANES, (p + 1) * LANES)
        vcols = slice(width + p * LANES, width + (p + 1) * LANES)
        datt = masked_ref[:, cols]
        query = query_ref[:, cols]
        dks, dvs, dqs = [], [], []
        for r in (slice(0, events), slice(events, 2 * events)):
            key = key_ref[p, r, :]
            if p < EARLY:
                weight, slope = weight_ref[p, r, :], slope_ref[p, r, :].astype(F32)
            else:
                weight, slope = silu_pair(nt(key, query))
            ds = (nt(value_ref[p, r, :], datt) * slope).astype(BF16)
            dks.append(nn(ds, query))
            dvs.append(nn(weight.astype(BF16), datt))
            dqs.append(nn(key.T, ds))
        dq_ref[:, cols] = (dqs[0] + dqs[1]).T.astype(BF16)
        dkv_ref[:, cols] = jnp.where(low, dks[0], dks[1]).astype(BF16)
        dkv_ref[:, vcols] = jnp.where(low, dvs[0], dvs[1]).astype(BF16)
    half = events // 2
    core = core_ref[0]
    mine = pl.ds(pl.multiple_of(core * half, half), half)
    other = pl.ds(pl.multiple_of((1 - core) * half, half), half)
    other_ref[...] = nt(dkv_ref[other, :], kvw_ref[...]).astype(BF16)
    mine_ref[...] = nt(dkv_ref[mine, :], kvw_ref[...])


def add_kernel(one_ref, two_ref, *rest):
    rest[-1][...] = (one_ref[...].astype(F32) + two_ref[...].astype(F32)).astype(BF16)


def final_kernel(core_ref, mine_ref, other_ref, part_ref, base_ref, weight_ref, out_hbm, result_ref, sems):
    half = mine_ref.shape[0]
    core = core_ref[0]
    mine = out_hbm.at[pl.ds(pl.multiple_of(core * half, half), half)]
    other = out_hbm.at[pl.ds(pl.multiple_of((1 - core) * half, half), half)]
    copies = start(sems, (mine_ref, mine), (other_ref, other))
    own, width = base_ref.shape
    parts = part_ref.shape[0] // own
    dq = jnp.sum(part_ref[...].astype(F32).reshape(parts, own, width), axis=0) * 0.0625
    result_ref[...] = (base_ref[...] + nt(dq.astype(BF16), weight_ref[...])).astype(BF16)
    for copy in copies:
        copy.wait()


def shards(
    history_embed,
    candidate_embed,
    query_weight,
    unit_weight,
    keyval_weight,
    output_weight,
    block_user,
    block_length,
    candidate_user,
    grad_output,
):
    own, width = candidate_embed.shape
    events = history_embed.shape[0]
    plane = lax.axis_size("plane")
    column = own * HIGH
    rows = column * plane
    s = jax.ShapeDtypeStruct

    def from_up(value, k):
        return lax.ppermute(value, "high", [((i + k) % HIGH, i) for i in range(HIGH)])

    def exchange(value):
        parts = value.reshape(plane, column, value.shape[-1])
        return lax.all_to_all(parts, "plane", 0, 0).reshape(rows, value.shape[-1])

    high = lax.axis_index("high").reshape(1)
    sems = pltpu.SemaphoreType.DMA
    full = width + LANES + width
    user = jnp.broadcast_to(candidate_user[:, None], (own, LANES)).astype(BF16)
    pack = jnp.concatenate([candidate_embed, user, grad_output], axis=1)
    wide = (s((PAIRS, 2 * events, LANES), BF16), "v")
    core = (lax.axis_index("cand") & 1).reshape(1)
    touched = call(touch_kernel, "v", [(s((16, LANES), BF16), "v")])(keyval_weight)[0]
    pay, spread = call(
        spread_kernel,
        "svvvvsssa",
        [(s((column, full), BF16), "v"), (s((plane, column, width + LANES), BF16), "v")],
    )(high, pack, *[from_up(pack, k) for k in (1, 2, 3)], block_user, block_length, core, touched)
    pay_all = exchange(spread)

    col_f32 = (s((column, width), F32), "v")
    col_b16 = (s((column, width), BF16), "v")
    own_f32 = (s((own, width), F32), "v")
    own_b16 = (s((own, width), BF16), "v")
    big = (s((rows, width), BF16), "v")
    gate, uslope, dgated = call(own_kernel, "vvv", [col_f32] * 3, flops=1 << 26)(
        pay, unit_weight, output_weight
    )
    keys, values, query, att = call(forward_kernel, "ssvvvv", [wide, wide, big, big], flops=1 << 31)(
        block_user, block_length, pay_all, query_weight, history_embed, keyval_weight
    )
    att_all = exchange(att)
    early = (s((EARLY, 2 * events, rows), BF16), "v")
    weight, slope = call(early_kernel, "vv", [early, early], flops=1 << 28)(query, keys)
    att_col = call(sum_kernel, "v", [col_b16], flops=1 << 20)(att_all)[0]
    datt, gated, dunit = call(
        norm_kernel, "s" + "v" * 7 + "a", [(s((plane, column, width), BF16), "v"), own_b16, own_b16], flops=1 << 20
    )(high, att_col, *[from_up(att_col, k) for k in (1, 2, 3)], gate, dgated, uslope, weight)
    datt_all = exchange(datt)
    candidate_output, base = call(output_kernel, "v" * 6, [own_b16, own_f32], flops=1 << 26)(
        candidate_embed, grad_output, gated, dunit, output_weight, unit_weight
    )
    half = events // 2
    half_b16 = (s((half, width), BF16), "v")
    dq, mine, other = call(
        backward_kernel,
        "ssvvvvvvvv",
        [big, (s((half, width), F32), "v"), half_b16],
        [pltpu.VMEM((rows, width), BF16), pltpu.VMEM((events, 2 * width), BF16)],
        flops=1 << 32,
    )(block_user, core, pay_all, query, datt_all, keys, values, keyval_weight, weight, slope)
    dq_all = lax.all_to_all(
        dq.reshape(plane * HIGH, own, width), ("plane", "high"), 0, 0
    ).reshape(rows, width)
    swap_core = [(i, i ^ 1) for i in range(4)]
    swap_chip = [(i, i ^ 2) for i in range(4)]
    got = lax.ppermute(other, "cand", swap_core)
    pair = call(add_kernel, "vv", [half_b16])(mine, got)[0]
    got = lax.ppermute(pair, "cand", swap_chip)
    quad = call(add_kernel, "vva", [half_b16])(pair, got, base)[0]
    got = lax.ppermute(quad, "cand", swap_core)
    history_grad, candidate_grad = call(
        final_kernel, "svvvvv", [(s((events, width), BF16), "h"), own_b16], [sems((2,))], flops=1 << 26
    )(core, quad, got, dq_all, base, query_weight)
    return (candidate_output, history_grad, candidate_grad)


def solution(mesh):
    seq, cand = mesh.shape["seq"], mesh.shape["cand"]
    fine = Mesh(mesh.devices.reshape(seq // HIGH, HIGH, cand), ("plane", "high", "cand"))
    hist, full = ("plane", "high"), ("plane", "high", "cand")
    in_specs = (
        P(hist, None),
        P(full, None),
        P(),
        P(),
        P(),
        P(),
        P(hist),
        P(hist),
        P(full),
        P(full, None),
    )
    out_specs = (P(full, None), P(hist, None), P(full, None))
    return jax.shard_map(shards, mesh=fine, in_specs=in_specs, out_specs=out_specs, check_vma=False)
```

```python
import jax
import jax.numpy as jnp
from jax import lax
from jax.experimental import pallas as pl
from jax.experimental.pallas import tpu as pltpu
from jax.sharding import Mesh, PartitionSpec as P

HEADS = 8
PAIRS = 4
LANES = 128
F32 = jnp.float32
BF16 = jnp.bfloat16
SMALL = 16 * 1024 * 1024
HIGH = 4
STEP = 256


def nn(a, b):
    return lax.dot_general(a, b, (((1,), (0,)), ((), ())), preferred_element_type=F32)


def nt(a, b):
    return lax.dot_general(a, b, (((1,), (1,)), ((), ())), preferred_element_type=F32)


def call(body, ins, outs, scratch=(), flops=0, limit=SMALL):
    place = {"v": pltpu.VMEM, "s": pltpu.SMEM, "h": pltpu.HBM, "a": pl.ANY}
    spec = [pl.BlockSpec(memory_space=place[i]) for i in ins]
    shapes = [shape for shape, _ in outs]
    out_spec = [pl.BlockSpec(memory_space=place[i]) for _, i in outs]
    return pl.pallas_call(
        body,
        out_shape=shapes,
        in_specs=spec,
        out_specs=out_spec,
        scratch_shapes=list(scratch),
        compiler_params=pltpu.CompilerParams(vmem_limit_bytes=limit),
        cost_estimate=pl.CostEstimate(flops=flops, bytes_accessed=1 << 20, transcendentals=0),
    )


def start(sems, *pairs):
    copies = [pltpu.make_async_copy(src, dst, sems.at[i]) for i, (src, dst) in enumerate(pairs)]
    for copy in copies:
        copy.start()
    return copies


def touch_kernel(ref, out_ref):
    out_ref[...] = ref[:16, :LANES]


def spread_kernel(high_ref, own_ref, one_ref, two_ref, three_ref, *rest):
    column_ref, plane_ref = rest[-2:]
    refs = (own_ref, one_ref, two_ref, three_ref)
    odd, upper = (high_ref[0] & 1) == 1, high_ref[0] >= 2
    a, b, c, d = [r[...].astype(F32) for r in refs]
    a, b, c, d = [jnp.where(odd, x, y) for x, y in ((b, a), (a, b), (d, c), (c, d))]
    a, b, c, d = [jnp.where(upper, x, y) for x, y in ((c, a), (d, b), (a, c), (b, d))]
    column = jnp.concatenate([a, b, c, d], axis=0).astype(BF16)
    column_ref[...] = column
    for i in range(plane_ref.shape[0]):
        plane_ref[i] = column[:, : plane_ref.shape[2]]


def put_keyval(length, hist_ref, weight_ref, key_ref, value_ref):
    events = hist_ref.shape[0]
    keyval = nn(hist_ref[...], weight_ref[...])
    row = lax.broadcasted_iota(jnp.int32, (events, LANES), 0)
    lane = lax.broadcasted_iota(jnp.int32, (events, LANES), 1)
    live = row < length
    half = LANES // 2
    for p in range(PAIRS):
        for ref, base in ((key_ref, 0), (value_ref, PAIRS * LANES)):
            part = keyval[:, base + p * LANES : base + (p + 1) * LANES]
            ref[p, :events, :] = jnp.where(live & (lane < half), part, 0.0).astype(BF16)
            ref[p, events:, :] = jnp.where(live & (lane >= half), part, 0.0).astype(BF16)


def forward_kernel(
    user_ref, length_ref, pay_ref, weight_ref, hist_ref, kvw_ref, key_ref, value_ref, query_ref, att_ref
):
    rows, width = query_ref.shape
    put_keyval(length_ref[0], hist_ref, kvw_ref, key_ref, value_ref)
    pay = pay_ref[...]
    mine = pay[:, width : width + 1].astype(F32) == user_ref[0].astype(F32)
    query = nn(pay[:, :width], weight_ref[...]).astype(BF16).astype(F32)
    query_ref[...] = jnp.where(mine, query * 0.0625, 0.0).astype(BF16)
    for p in range(PAIRS):
        cols = slice(p * LANES, (p + 1) * LANES)
        for r in range(0, rows, STEP):
            r = slice(r, r + STEP)
            u = nt(query_ref[r, cols], key_ref[p])
            w = (u + u * jnp.tanh(u)).astype(BF16)
            att_ref[r, cols] = nn(w, value_ref[p]).astype(BF16)


def own_kernel(pay_ref, unit_ref, out_ref, gate_ref, uslope_ref, dgated_ref):
    width = unit_ref.shape[0]
    pay = pay_ref[...]
    linear = nn(pay[:, :width], unit_ref[...])
    sig = jax.nn.sigmoid(linear)
    gate_ref[...] = (linear * sig).astype(BF16).astype(F32)
    uslope_ref[...] = sig * (1.0 + linear * (1.0 - sig))
    dgated_ref[...] = nt(pay[:, width + LANES :], out_ref[...])


def sum_kernel(part_ref, out_ref):
    own, width = out_ref.shape
    parts = part_ref.shape[0] // own
    total = jnp.sum(part_ref[...].astype(F32).reshape(parts, own, width), axis=0)
    out_ref[...] = total.astype(out_ref.dtype)


def norm_kernel(
    high_ref, own_ref, one_ref, two_ref, three_ref, gate_ref, dgated_ref, uslope_ref, datt_ref, gated_ref, dunit_ref
):
    own, width = gate_ref.shape
    block = own // HIGH
    refs = (own_ref, one_ref, two_ref, three_ref)
    att = sum(ref[...].astype(F32) for ref in refs)
    mean = jnp.mean(att, axis=1, keepdims=True)
    centered = att - mean
    inverse = lax.rsqrt(jnp.mean(centered * centered, axis=1, keepdims=True) + 1e-05)
    normed = centered * inverse
    gate = gate_ref[...]
    dgated = dgated_ref[...]
    g = dgated * gate
    datt = inverse * (
        g
        - jnp.mean(g, axis=1, keepdims=True)
        - normed * jnp.mean(g * normed, axis=1, keepdims=True)
    )
    datt = datt.astype(BF16)
    for i in range(datt_ref.shape[0]):
        datt_ref[i] = datt
    down = ((HIGH - high_ref[0]) & (HIGH - 1)) * block
    gated_ref[...] = pltpu.roll(normed * gate, down, 0)[:block].astype(BF16)
    dunit_ref[...] = pltpu.roll(dgated * normed * uslope_ref[...], down, 0)[:block].astype(BF16)


def output_kernel(embed_ref, grad_ref, gated_ref, dunit_ref, out_ref, unit_ref, result_ref, base_ref):
    result_ref[...] = (embed_ref[...].astype(F32) + nn(gated_ref[...], out_ref[...])).astype(BF16)
    base_ref[...] = grad_ref[...].astype(F32) + nt(dunit_ref[...], unit_ref[...])


def silu_pair(u):
    t = jnp.tanh(u)
    ut = u * t
    return u + ut, (1.0 + t) + (u - ut * t)


def backward_kernel(
    user_ref, core_ref, pay_ref, query_ref, datt_ref, key_ref, value_ref, kvw_ref,
    dq_ref, mine_ref, other_ref, masked_ref, dkv_ref,
):
    width = datt_ref.shape[1]
    events = value_ref.shape[1] // 2
    owned = pay_ref[...][:, width : width + 1].astype(F32) == user_ref[0].astype(F32)
    masked_ref[...] = jnp.where(owned, datt_ref[...].astype(F32), 0.0).astype(BF16)
    low = lax.broadcasted_iota(jnp.int32, (events, LANES), 1) < LANES // 2
    for p in range(PAIRS):
        cols = slice(p * LANES, (p + 1) * LANES)
        vcols = slice(width + p * LANES, width + (p + 1) * LANES)
        datt = masked_ref[:, cols]
        query = query_ref[:, cols]
        dks, dvs, dqs = [], [], []
        for r in (slice(0, events), slice(events, 2 * events)):
            key = key_ref[p, r, :]
            weight, slope = silu_pair(nt(key, query))
            ds = (nt(value_ref[p, r, :], datt) * slope).astype(BF16)
            dks.append(nn(ds, query))
            dvs.append(nn(weight.astype(BF16), datt))
            dqs.append(nn(key.T, ds))
        dq_ref[:, cols] = (dqs[0] + dqs[1]).T.astype(BF16)
        dkv_ref[:, cols] = jnp.where(low, dks[0], dks[1]).astype(BF16)
        dkv_ref[:, vcols] = jnp.where(low, dvs[0], dvs[1]).astype(BF16)
    half = events // 2
    core = core_ref[0]
    mine = pl.ds(pl.multiple_of(core * half, half), half)
    other = pl.ds(pl.multiple_of((1 - core) * half, half), half)
    other_ref[...] = nt(dkv_ref[other, :], kvw_ref[...]).astype(BF16)
    mine_ref[...] = nt(dkv_ref[mine, :], kvw_ref[...])


def add_kernel(one_ref, two_ref, *rest):
    rest[-1][...] = (one_ref[...].astype(F32) + two_ref[...].astype(F32)).astype(BF16)


def halves_kernel(core_ref, mine_ref, other_ref, out_hbm, sems):
    half = mine_ref.shape[0]
    core = core_ref[0]
    mine = out_hbm.at[pl.ds(pl.multiple_of(core * half, half), half)]
    other = out_hbm.at[pl.ds(pl.multiple_of((1 - core) * half, half), half)]
    for copy in start(sems, (mine_ref, mine), (other_ref, other)):
        copy.wait()


def final_kernel(part_ref, base_ref, weight_ref, result_ref):
    own, width = base_ref.shape
    parts = part_ref.shape[0] // own
    dq = jnp.sum(part_ref[...].astype(F32).reshape(parts, own, width), axis=0) * 0.0625
    result_ref[...] = (base_ref[...] + nt(dq.astype(BF16), weight_ref[...])).astype(BF16)


def shards(
    history_embed,
    candidate_embed,
    query_weight,
    unit_weight,
    keyval_weight,
    output_weight,
    block_user,
    block_length,
    candidate_user,
    grad_output,
):
    own, width = candidate_embed.shape
    events = history_embed.shape[0]
    plane = lax.axis_size("plane")
    column = own * HIGH
    rows = column * plane
    s = jax.ShapeDtypeStruct

    def from_up(value, k):
        return lax.ppermute(value, "high", [(i ^ k, i) for i in range(HIGH)])

    def exchange(value):
        parts = value.reshape(plane, column, value.shape[-1])
        return lax.all_to_all(parts, "plane", 0, 0).reshape(rows, value.shape[-1])

    high = lax.axis_index("high").reshape(1)
    sems = pltpu.SemaphoreType.DMA
    full = width + LANES + width
    user = jnp.broadcast_to(candidate_user[:, None], (own, LANES)).astype(BF16)
    pack = jnp.concatenate([candidate_embed, user, grad_output], axis=1)
    wide = (s((PAIRS, 2 * events, LANES), BF16), "v")
    core = (lax.axis_index("cand") & 1).reshape(1)
    touched = call(touch_kernel, "v", [(s((16, LANES), BF16), "v")])(keyval_weight)[0]
    pay, spread = call(
        spread_kernel,
        "svvvvsssa",
        [(s((column, full), BF16), "v"), (s((plane, column, width + LANES), BF16), "v")],
    )(high, pack, *[from_up(pack, k) for k in (1, 2, 3)], block_user, block_length, core, touched)
    pay_all = exchange(spread)

    col_f32 = (s((column, width), F32), "v")
    col_b16 = (s((column, width), BF16), "v")
    own_f32 = (s((own, width), F32), "v")
    own_b16 = (s((own, width), BF16), "v")
    big = (s((rows, width), BF16), "v")
    gate, uslope, dgated = call(own_kernel, "vvv", [col_f32] * 3, flops=1 << 26)(
        pay, unit_weight, output_weight
    )
    keys, values, query, att = call(forward_kernel, "ssvvvv", [wide, wide, big, big], flops=1 << 31)(
        block_user, block_length, pay_all, query_weight, history_embed, keyval_weight
    )
    att_all = exchange(att)
    att_col = call(sum_kernel, "v", [col_b16], flops=1 << 20)(att_all)[0]
    datt, gated, dunit = call(
        norm_kernel, "s" + "v" * 7, [(s((plane, column, width), BF16), "v"), own_b16, own_b16], flops=1 << 20
    )(high, att_col, *[from_up(att_col, k) for k in (1, 2, 3)], gate, dgated, uslope)
    datt_all = exchange(datt)
    candidate_output, base = call(output_kernel, "v" * 6, [own_b16, own_f32], flops=1 << 26)(
        candidate_embed, grad_output, gated, dunit, output_weight, unit_weight
    )
    half = events // 2
    half_b16 = (s((half, width), BF16), "v")
    dq, mine, other = call(
        backward_kernel,
        "ssvvvvvv",
        [big, (s((half, width), F32), "v"), half_b16],
        [pltpu.VMEM((rows, width), BF16), pltpu.VMEM((events, 2 * width), BF16)],
        flops=1 << 32,
    )(block_user, core, pay_all, query, datt_all, keys, values, keyval_weight)
    dq_all = lax.all_to_all(
        dq.reshape(plane * HIGH, own, width), ("plane", "high"), 0, 0
    ).reshape(rows, width)
    swap_core = [(i, i ^ 1) for i in range(4)]
    swap_chip = [(i, i ^ 2) for i in range(4)]
    got = lax.ppermute(other, "cand", swap_core)
    pair = call(add_kernel, "vv", [half_b16])(mine, got)[0]
    got = lax.ppermute(pair, "cand", swap_chip)
    quad = call(add_kernel, "vv", [half_b16])(pair, got)[0]
    got = lax.ppermute(quad, "cand", swap_core)
    history_grad = call(halves_kernel, "svv", [(s((events, width), BF16), "h")], [sems((2,))])(
        core, quad, got
    )[0]
    candidate_grad = call(final_kernel, "v" * 3, [own_b16], flops=1 << 26)(dq_all, base, query_weight)[0]
    return (candidate_output, history_grad, candidate_grad)


def solution(mesh):
    seq, cand = mesh.shape["seq"], mesh.shape["cand"]
    fine = Mesh(mesh.devices.reshape(seq // HIGH, HIGH, cand), ("plane", "high", "cand"))
    hist, full = ("plane", "high"), ("plane", "high", "cand")
    in_specs = (
        P(hist, None),
        P(full, None),
        P(),
        P(),
        P(),
        P(),
        P(hist),
        P(hist),
        P(full),
        P(full, None),
    )
    out_specs = (P(full, None), P(hist, None), P(full, None))
    return jax.shard_map(shards, mesh=fine, in_specs=in_specs, out_specs=out_specs, check_vma=False)
```
